128 devices in a mesh: slide: 16 (over z_hi, x, core), ctx: 8 (over y, z_lo).
Axes of the slice: x: 4, y: 4, z: 4 (z_hi: 2, z_lo: 2; z = z_hi * 2 + z_lo), core: 2. Of those that a mesh axis runs over, the one named last changes fastest.
Arguments:
- tile_rows: bfloat16 [65536, 768], P(('slide', 'ctx')), may hold values from -6 to 6
- tile_slot: int32 [128, 512], P(('slide', 'ctx')), may hold values from 0 to 65535, as said below
- lengths: int32 [16], P('slide'), may hold values from 1365 to 4096, as said below
- ln_gain_attn: float32 [768], replicated, may hold values from 0.5 to 1.5
- w_query: bfloat16 [768, 768], P('slide'), may hold values from -1 to 1
- w_kv: bfloat16 [768, 1536], P('slide'), may hold values from -2 to 2
- w_out: bfloat16 [768, 768], P('slide'), may hold values from -0.21875 to 0.21875
- ln_gain_mlp: float32 [768], replicated, may hold values from 0.5 to 1.5
- w_up: bfloat16 [768, 3072], P('slide'), may hold values from -0.21875 to 0.21875
- w_down: bfloat16 [3072, 768], P('slide'), may hold values from -0.109375 to 0.109375
Outputs:
- encoded: bfloat16 [65536, 768], P(('slide', 'ctx'))
The draws below stay inside these ranges and needn't reach their ends.
Inputs may be any that keep to these rules, and one draw needn't show every extreme that they name: `tile_slot`: over all devices every row number 0 to 65535 appears exactly once; the entries on each device include exactly 4 rows of the block of 512 rows of each device, devices ordered by slide and then ctx. `lengths`: some slide has exactly 4096 tiles.
All inputs are finite; a program needn't handle non-finite values.
Results may differ from the reference program's by a relative error of at most 0.009.
Values may be sent and summed in bfloat16 or wider, within the bound.
A program may use at most 256 MiB of HBM per device.

```python
import math
import jax
import jax.numpy as jnp
from jax import lax

D = 768
HEADS = 12
HEAD_DIM = 64
FF = 3072
BLOCK = 512
SEQ = 4096
SLIDES = 16
N_SLIDE = 16
N_CTX = 8


def shared_base(key):
    return jnp.clip(jax.random.normal(key, (D, D), jnp.float32), -3.0, 3.0)


def draw_w_query(key, part):
    base = shared_base(key)
    return (base * (2.5 / math.sqrt(D))).astype(jnp.bfloat16)


def draw_w_kv(key, part):
    key = jax.random.fold_in(key, 7)
    first_key = jax.random.fold_in(key, 0)
    fresh = jnp.clip(jax.random.normal(first_key, (D, 2 * D), jnp.float32), -3.0, 3.0) / math.sqrt(D)
    return fresh.astype(jnp.bfloat16)


def draw_lengths(key, part):
    key = jax.random.fold_in(key, 13)
    first_key, second_key = jax.random.split(key)
    drawn = jax.random.randint(first_key, (N_SLIDE,), SEQ // 3, SEQ + 1)
    longest = jax.random.randint(second_key, (), 0, N_SLIDE)
    return jnp.where(jnp.arange(N_SLIDE) == longest, SEQ, drawn).astype(jnp.int32)


def one_permutation(key):
    return jax.random.permutation(key, BLOCK)


def draw_tile_slot(key, part):
    key = jax.random.fold_in(key, 11)
    device_count = N_SLIDE * N_CTX
    pair_rows = BLOCK // device_count
    first_key, second_key = jax.random.split(key)
    spread = jax.vmap(one_permutation)(jax.random.split(first_key, device_count))
    slots = jnp.arange(device_count, dtype=jnp.int32)[:, None] * BLOCK + spread.astype(jnp.int32)
    by_source = slots.reshape(device_count, device_count, pair_rows).transpose(1, 0, 2).reshape(device_count, BLOCK)
    shuffles = jax.vmap(one_permutation)(jax.random.split(second_key, device_count))
    return jnp.take_along_axis(by_source, shuffles, axis=1).astype(jnp.int32)


def block_levels(key, extent, shards, smallest, top_value):
    loudness, own = 1.0, jax.random.fold_in(key, 6)
    for axis_at, parts in shards:
        draws = jnp.exp(jax.random.uniform(jax.random.fold_in(own, axis_at), (parts,), jnp.float32, smallest / len(shards), top_value / len(shards)))
        loudness = loudness * jnp.repeat(draws, extent[axis_at] // parts).reshape([-1 if axis == axis_at else 1 for axis in range(len(extent))])
    return loudness


def scatter_about(rng, dims, scale, limit, pieces=(), kind=jnp.bfloat16):
    array = scale * jax.random.normal(rng, dims, jnp.float32)
    if pieces:
        array = array * block_levels(rng, dims, pieces, -0.22, 0.18)
    return jnp.clip(array, -limit, limit).astype(kind)


def setup_inputs(seed: int = 0) -> dict:
    splits = jax.random.split(jax.random.key(seed), 11)
    tile_rows = scatter_about(splits[0], (N_SLIDE * N_CTX * BLOCK, D), 1.0, 6.0, ((0, 128),))
    tile_slot = draw_tile_slot(jax.random.fold_in(splits[10], 71), 0)
    lengths = draw_lengths(jax.random.fold_in(splits[10], 71), 0)
    ln_gain_attn = jnp.clip(1.0 + 0.1 * jax.random.normal(splits[3], (D,), jnp.float32), 0.5, 1.5)
    w_query = draw_w_query(jax.random.fold_in(splits[10], 71), 0)
    w_kv = draw_w_kv(jax.random.fold_in(splits[10], 71), 0)
    w_out = scatter_about(splits[6], (D, D), D ** -0.5, 0.21875, ((0, 16),))
    ln_gain_mlp = jnp.clip(1.0 + 0.1 * jax.random.normal(splits[7], (D,), jnp.float32), 0.5, 1.5)
    w_up = scatter_about(splits[8], (D, FF), D ** -0.5, 0.21875, ((0, 16),))
    w_down = scatter_about(splits[9], (FF, D), FF ** -0.5, 0.109375, ((0, 16),))
    return dict(tile_rows=tile_rows, tile_slot=tile_slot, lengths=lengths, ln_gain_attn=ln_gain_attn, w_query=w_query, w_kv=w_kv, w_out=w_out, ln_gain_mlp=ln_gain_mlp, w_up=w_up, w_down=w_down)


norm_eps = 1e-05
masked_score = -1e+30

def stored(array_in):
    return lax.optimization_barrier(array_in.astype(jnp.bfloat16))

def layer_norm(rows, gain):
    values32 = rows.astype(jnp.float32)
    row_mean = lax.optimization_barrier(jnp.mean(values32, axis=-1, keepdims=True))
    centred = values32 - row_mean
    row_var = lax.optimization_barrier(jnp.mean(centred * centred, axis=-1, keepdims=True))
    return stored(centred * lax.rsqrt(row_var + norm_eps) * gain)

def slide_layer(rows, length, ln_gain_attn, w_query, w_kv, w_out, ln_gain_mlp, w_up, w_down):
    normed = layer_norm(rows, ln_gain_attn)
    query = stored(jnp.dot(normed, w_query, preferred_element_type=jnp.float32))
    keyval = stored(jnp.dot(normed, w_kv, preferred_element_type=jnp.float32))
    key_heads = keyval[:, :D].reshape(SEQ, HEADS, HEAD_DIM).astype(jnp.float32)
    value_heads = keyval[:, D:].reshape(SEQ, HEADS, HEAD_DIM).astype(jnp.float32)
    positions = jnp.arange(SEQ, dtype=jnp.int32)
    key_valid = positions < length
    query_blocks = query.reshape(N_CTX, BLOCK, HEADS, HEAD_DIM)

    def attend_block(query_block):
        scores = jnp.einsum('qhd,khd->hqk', query_block.astype(jnp.float32), key_heads) * HEAD_DIM ** (-0.5)
        scores = jnp.where(key_valid[None, None, :], scores, masked_score)
        row_max = lax.optimization_barrier(jnp.max(scores, axis=-1, keepdims=True))
        weights = jnp.exp(scores - row_max)
        total = lax.optimization_barrier(jnp.sum(weights, axis=-1))
        weights_bf = stored(weights).astype(jnp.float32)
        summed = jnp.einsum('hqk,khd->qhd', weights_bf, value_heads)
        return (summed / jnp.transpose(total)[:, :, None]).reshape(BLOCK, D).astype(jnp.bfloat16)
    attended = lax.map(attend_block, query_blocks).reshape(SEQ, D)
    mid = stored(rows.astype(jnp.float32) + jnp.dot(attended, w_out, preferred_element_type=jnp.float32))
    normed_mlp = layer_norm(mid, ln_gain_mlp)
    hidden = stored(jax.nn.gelu(jnp.dot(normed_mlp, w_up, preferred_element_type=jnp.float32)))
    encoded = mid.astype(jnp.float32) + jnp.dot(hidden, w_down, preferred_element_type=jnp.float32)
    return jnp.where(key_valid[:, None], encoded, 0.0).astype(jnp.bfloat16)

def reference(tile_rows, tile_slot, lengths, ln_gain_attn, w_query, w_kv, w_out, ln_gain_mlp, w_up, w_down):
    ordering = jnp.argsort(tile_slot.reshape(-1)).astype(jnp.int32)
    seq_rows = tile_rows[ordering].reshape(SLIDES, SEQ, D)

    def one_slide(inputs):
        rows, length = inputs
        return slide_layer(rows, length, ln_gain_attn, w_query, w_kv, w_out, ln_gain_mlp, w_up, w_down)
    encoded = lax.map(one_slide, (seq_rows, lengths))
    return encoded.reshape(SLIDES * SEQ, D)
```

```python
import functools

import jax
import jax.numpy as jnp
from jax import lax
from jax.experimental import pallas as pl
from jax.experimental.pallas import tpu as pltpu
from jax.sharding import PartitionSpec as P

HEAD_DIM = 64
MESH = pl.DeviceIdType.MESH
bf16, f32 = jnp.bfloat16, jnp.float32

norm_eps = 1e-05
masked_score = -1e30
value_rows = 80
ORDER = [
    (0, 0), (0, 1), (1, 0), (2, 0), (3, 0), (1, 1), (2, 1), (3, 1),
    (6, 0), (5, 0), (6, 1), (4, 0), (7, 0), (4, 1), (5, 1), (7, 1),
]


def layer_norm(rows, gain):
    values32 = rows.astype(f32)
    row_mean = jnp.mean(values32, axis=-1, keepdims=True)
    centred = values32 - row_mean
    row_var = jnp.mean(centred * centred, axis=-1, keepdims=True)
    return (centred * lax.rsqrt(row_var + norm_eps) * gain).astype(bf16)


def dot(left, right):
    return jnp.dot(left, right, preferred_element_type=f32)


def dot_nt(left, right):
    return lax.dot_general(left, right, (((1,), (1,)), ((), ())), preferred_element_type=f32)


def identity(size):
    row = lax.broadcasted_iota(jnp.int32, (size, size), 0)
    column = lax.broadcasted_iota(jnp.int32, (size, size), 1)
    return jnp.where(row == column, 1.0, 0.0).astype(bf16)


def layer_kernel(
    tok, length_ref, gain1, wq, wkv, wo, gain2, wu, wd,
    out,
    rows, w_a, w_b, w_c, w_vt, q_aug, k_buf, v_buf, bias, scores, top, acc, attended, up_buf, down_acc,
    t_send, t_recv, a_send, a_recv, b_send, b_recv, c_send, c_recv,
):
    block, width = tok.shape
    half = block // 2
    heads = width // HEAD_DIM
    pairs = heads // 2
    hidden = wu.shape[1]
    slide = lax.axis_index("slide")
    ctx = lax.axis_index("ctx")
    z_hi, x, core = lax.div(slide, 8), lax.rem(lax.div(slide, 2), 4), lax.rem(slide, 2)
    y, z_lo = lax.div(ctx, 2), lax.rem(ctx, 2)

    def at_slide(zz, xx, cc):
        return zz * 8 + lax.rem(xx + 4, 4) * 2 + cc

    def at_ctx(yy, zz):
        return lax.rem(yy + 4, 4) * 2 + zz

    y_next = (slide, at_ctx(y + 1, z_lo))
    y_prev = (slide, at_ctx(y - 1, z_lo))
    z_pair = (slide, at_ctx(y, 1 - z_lo))
    x_next = (at_slide(z_hi, x + 1, core), ctx)
    x_prev = (at_slide(z_hi, x - 1, core), ctx)
    zw_pair = (at_slide(1 - z_hi, x, core), at_ctx(y, 1 - z_lo))
    sibling = (at_slide(z_hi, x, 1 - core), ctx)

    barrier = pltpu.get_barrier_semaphore()
    for peer in (y_next, y_prev, z_pair, x_next, x_prev, zw_pair, sibling):
        pl.semaphore_signal(barrier, inc=1, device_id=peer, device_id_type=MESH)
    pl.semaphore_wait(barrier, 7)

    def shard_of(relation, cc):
        zz = (1 - z_hi) if relation in (3, 4, 5, 7) else z_hi
        step = {0: 0, 1: -1, 2: 1, 3: 0, 4: -1, 5: 1, 6: 2, 7: 2}[relation]
        return at_slide(zz, x + step, cc)

    class Gather:
        def __init__(self, whole, depth, send, recv):
            self.whole, self.depth, self.send, self.recv = whole, depth, send, recv
            self.started = []

        def part(self, relation, cc, side=None):
            at = pl.ds(pl.multiple_of(shard_of(relation, cc) * self.depth, 16), self.depth)
            if side is None:
                return self.whole.at[at, :]
            cut = self.whole.shape[1] // 2
            return self.whole.at[at, pl.ds(side * cut, cut)]

        def handle(self, key, send_slot, slot, peer):
            part = self.part(*key)
            return pltpu.make_async_remote_copy(
                src_ref=part, dst_ref=part, send_sem=self.send.at[send_slot],
                recv_sem=self.recv.at[slot], device_id=peer, device_id_type=MESH,
            )

        def copy(self, key, peer, slot):
            self.handle(key, len(self.started), slot, peer).start()
            self.started.append(key)

        def arrive(self, key, slot):
            self.handle(key, 0, slot, sibling).wait_recv()

        def first(self):
            own = (0, core)
            self.copy(own, x_next, 1)
            self.copy(own, x_prev, 2)
            self.copy(own, zw_pair, 3)
            self.copy(own, sibling, 8)

        def second(self):
            for relation in (1, 2, 3):
                self.arrive((relation, core), relation)
            self.copy((1, core, 0), x_next, 6)
            self.copy((2, core, 1), x_prev, 0)
            self.copy((3, core), x_next, 4)
            self.copy((3, core), x_prev, 5)
            for relation in (1, 2, 3):
                self.copy((relation, core), sibling, 8 + relation)

        def third(self):
            self.arrive((6, core, 0), 6)
            self.arrive((6, core, 1), 0)
            self.copy((6, core), zw_pair, 7)
            self.copy((6, core), sibling, 14)

        def fourth(self):
            for relation in (4, 5, 7):
                self.arrive((relation, core), relation)
                self.copy((relation, core), sibling, 8 + relation)

        def last(self):
            for relation in range(8):
                self.arrive((relation, 1 - core), 8 + relation)

        def sent(self):
            for index, key in enumerate(self.started):
                self.handle(key, index, 0, sibling).wait_send()

    gather_a = Gather(w_a, wq.shape[0], a_send, a_recv)
    gather_b = Gather(w_b, wu.shape[0], b_send, b_recv)
    gather_c = Gather(w_c, wd.shape[0], c_send, c_recv)

    own48 = pl.ds(pl.multiple_of(slide * wq.shape[0], 16), wq.shape[0])
    w_a[own48, 0:width] = wq[...]
    w_a[own48, width:] = wkv[...]
    gather_a.first()

    place = {key: index for index, key in enumerate(ORDER)}

    def chunk(relation, side):
        return rows.at[pl.ds(place[relation, side] * half, half), :]

    token_sends = []

    def rows_handle(source, target, send_slot, peer):
        return pltpu.make_async_remote_copy(
            src_ref=chunk(*source), dst_ref=chunk(*target), send_sem=t_send.at[send_slot],
            recv_sem=t_recv.at[place[target]], device_id=peer, device_id_type=MESH,
        )

    def pass_rows(source, relation, side, peer):
        rows_handle(source, (relation, side), len(token_sends), peer).start()
        token_sends.append(source)

    def rows_here(relation, side):
        rows_handle((relation, side), (relation, side), 0, sibling).wait_recv()

    for side in range(2):
        rows[side * half : (side + 1) * half, :] = layer_norm(
            tok[side * half : (side + 1) * half, :], gain1[...]
        )
        pass_rows((0, side), 1, side, y_next)
        pass_rows((0, side), 2, side, y_prev)
        pass_rows((0, side), 3, side, z_pair)

    w_b[own48, 0:width] = wo[...]
    w_b[own48, width:] = wu[...]
    own192 = pl.ds(pl.multiple_of(slide * wd.shape[0], 16), wd.shape[0])
    w_c[own192, :] = wd[...]

    q_aug[...] = jnp.zeros(q_aug.shape, bf16)
    q_aug[:, 128:144, :] = jnp.where(
        lax.broadcasted_iota(jnp.int32, (pairs, 16, 2 * block), 1) == 0, 1.0, 0.0
    ).astype(bf16)
    v_buf[:, 64:80, :] = jnp.where(
        lax.broadcasted_iota(jnp.int32, (heads, 16, block), 1) == 0, 1.0, 0.0
    ).astype(bf16)
    top[...] = jnp.full(top.shape, masked_score, f32)
    acc[...] = jnp.zeros(acc.shape, f32)

    gather_a.second()
    gather_a.third()
    for relation in (1, 2, 3):
        rows_here(relation, 0)
    pass_rows((1, 0), 6, 0, y_next)
    pass_rows((3, 0), 5, 0, y_prev)
    pass_rows((3, 0), 4, 0, y_next)
    gather_a.fourth()
    gather_b.first()
    gather_a.last()

    scale = HEAD_DIM ** (-0.5) * 1.4426950408889634
    queries = (dot(rows[0:block, :], w_a[:, 0:width]) * scale).astype(bf16)
    queries_t = dot_nt(identity(width), queries).astype(bf16)
    for head in range(heads):
        pair, at = head // 2, head % 2
        q_aug[pair, at * 64 : at * 64 + 64, at * block : (at + 1) * block] = queries_t[
            head * 64 : head * 64 + 64, :
        ]
    w_vt[...] = dot_nt(identity(width), w_a[:, 2 * width :]).astype(bf16)

    length = length_ref[0]

    def position(relation, side):
        step = {0: 0, 1: -1, 2: 1, 3: 0, 4: -1, 5: 1, 6: 2, 7: 2}[relation]
        zz = (1 - z_lo) if relation in (3, 4, 5, 7) else z_lo
        return at_ctx(y + step, zz) * block + side * half

    def attend(step, first, second):
        here = rows[pl.ds(pl.multiple_of(step * block, block), block), :]
        k_buf[...] = dot(here, w_a[:, width : 2 * width]).astype(bf16)
        values_t = dot_nt(w_vt[...], here).astype(bf16)
        for head in range(heads):
            v_buf[head, 0:64, :] = values_t[head * 64 : head * 64 + 64, :]
        line = lax.broadcasted_iota(jnp.int32, (block, 128), 0)
        lane = lax.broadcasted_iota(jnp.int32, (block, 128), 1)
        at = jnp.where(line < half, first + line, second + line - half)
        bias[...] = jnp.where((lane == 0) & (at >= length), masked_score, 0.0).astype(bf16)

        def score(pair, slot):
            keys = k_buf[:, pl.ds(pl.multiple_of(pair * 128, 128), 128)]
            scores[slot] = dot(jnp.concatenate([keys, bias[...]], axis=1), q_aug[pair])

        def soften(pair, slot):
            before = top[pair]
            now = jnp.maximum(before, jnp.max(scores[slot], axis=0, keepdims=True))
            factor = jnp.exp2(before - now)
            top[pair] = now
            for side in range(2):
                span = slice(side * block, (side + 1) * block)
                weights = jnp.exp2(scores[slot, :, span] - now[:, span]).astype(bf16)
                head = 2 * pair + side
                acc[head] = acc[head] * factor[:, span] + dot(v_buf[head], weights)

        score(0, 0)

        def two(index, _):
            score(2 * index + 1, 1)
            soften(2 * index, 0)
            score(jnp.minimum(2 * index + 2, pairs - 1), 0)
            soften(2 * index + 1, 1)
            return 0

        lax.fori_loop(0, pairs // 2, two, 0)

    steps = len(ORDER) // 2
    firsts = [position(*ORDER[2 * step]) for step in range(steps)]
    seconds = [position(*ORDER[2 * step + 1]) for step in range(steps)]

    def pick(options, step):
        chosen = options[0]
        for index in range(1, len(options)):
            chosen = jnp.where(step == index, options[index], chosen)
        return chosen

    def turn(step, _):
        @pl.when(step == 2)
        def _():
            for relation in (1, 2, 3):
                rows_here(relation, 1)
            pass_rows((3, 1), 4, 1, y_next)
            pass_rows((2, 1), 6, 1, y_prev)
            pass_rows((3, 1), 5, 1, y_prev)
            gather_b.second()

        @pl.when(step == 3)
        def _():
            gather_b.third()
            gather_c.first()

        @pl.when(step == 4)
        def _():
            rows_here(6, 0)
            pass_rows((6, 0), 7, 0, z_pair)
            rows_here(5, 0)
            gather_b.fourth()

        @pl.when(step == 5)
        def _():
            rows_here(6, 1)
            pass_rows((6, 1), 7, 1, z_pair)
            rows_here(4, 0)
            gather_c.second()

        @pl.when(step == 6)
        def _():
            rows_here(7, 0)
            rows_here(4, 1)
            gather_c.third()

        @pl.when(step == 7)
        def _():
            rows_here(5, 1)
            rows_here(7, 1)
            gather_c.fourth()

        attend(step, pick(firsts, step), pick(seconds, step))
        return 0

    lax.fori_loop(0, steps, turn, 0)

    gather_b.last()
    for head in range(heads):
        done = acc[head]
        attended[head * 64 : head * 64 + 64, :] = (done[0:64] / done[64:65]).astype(bf16)
    turned = dot_nt(identity(block), attended[...]).astype(bf16)
    mid = (tok[...].astype(f32) + dot(turned, w_b[:, 0:width])).astype(bf16)
    for index, source in enumerate(token_sends):
        rows_handle(source, source, index, sibling).wait_send()
    rows[0:block, :] = layer_norm(mid, gain2[...])
    gather_c.last()
    down_acc[...] = mid.astype(f32)

    tile = up_buf.shape[2]
    tiles = hidden // tile

    def up(index, slot):
        at = pl.ds(pl.multiple_of(width + index * tile, 128), tile)
        up_buf[slot] = dot(rows[0:block, :], w_b[:, at])

    def down(index, slot):
        active = jax.nn.gelu(up_buf[slot], approximate=True).astype(bf16)
        down_acc[...] += dot(active, w_c[pl.ds(pl.multiple_of(index * tile, tile), tile), :])

    up(0, 0)

    def two_tiles(index, _):
        up(2 * index + 1, 1)
        down(2 * index, 0)
        up(jnp.minimum(2 * index + 2, tiles - 1), 0)
        down(2 * index + 1, 1)
        return 0

    lax.fori_loop(0, tiles // 2, two_tiles, 0)
    at = ctx * block + lax.broadcasted_iota(jnp.int32, (block, width), 0)
    out[...] = jnp.where(at < length, down_acc[...], 0.0).astype(bf16)

    for gather in (gather_a, gather_b, gather_c):
        gather.sent()


def layer(tokens, lengths, gain1, wq, wkv, wo, gain2, wu, wd):
    block, width = tokens.shape
    heads = width // HEAD_DIM
    hidden = wu.shape[1]
    slides = lax.axis_size("slide")
    vmem = pl.BlockSpec(memory_space=pltpu.VMEM)
    dma = pltpu.SemaphoreType.DMA
    return pl.pallas_call(
        layer_kernel,
        out_shape=jax.ShapeDtypeStruct((block, width), bf16),
        in_specs=[vmem, pl.BlockSpec(memory_space=pltpu.SMEM)] + [vmem] * 7,
        out_specs=vmem,
        scratch_shapes=[
            pltpu.VMEM((8 * block, width), bf16),
            pltpu.VMEM((width, 3 * width), bf16),
            pltpu.VMEM((width, width + hidden), bf16),
            pltpu.VMEM((hidden, width), bf16),
            pltpu.VMEM((width, width), bf16),
            pltpu.VMEM((heads // 2, 256, 2 * block), bf16),
            pltpu.VMEM((block, width), bf16),
            pltpu.VMEM((heads, value_rows, block), bf16),
            pltpu.VMEM((block, 128), bf16),
            pltpu.VMEM((2, block, 2 * block), f32),
            pltpu.VMEM((heads // 2, 1, 2 * block), f32),
            pltpu.VMEM((heads, value_rows, block), f32),
            pltpu.VMEM((width, block), bf16),
            pltpu.VMEM((2, block, 512), f32),
            pltpu.VMEM((block, width), f32),
            dma((14,)), dma((16,)),
            dma((16,)), dma((16,)),
            dma((16,)), dma((16,)),
            dma((16,)), dma((16,)),
        ],
        compiler_params=pltpu.CompilerParams(
            collective_id=0, has_side_effects=True, vmem_limit_bytes=60 * 2**20
        ),
        name="layer",
    )(tokens, lengths, gain1.reshape(1, width), wq, wkv, wo, gain2.reshape(1, width), wu, wd)


def on_device(
    tile_rows, tile_slot, lengths, ln_gain_attn, w_query, w_kv, w_out, ln_gain_mlp, w_up, w_down
):
    block_rows, model_width = tile_rows.shape
    device_count = lax.axis_size(("slide", "ctx"))
    pair_rows = block_rows // device_count
    slot_ids = tile_slot[0]
    owners = slot_ids // block_rows
    ordering = jnp.argsort(owners, stable=True)
    outgoing = tile_rows[ordering].reshape(device_count, pair_rows, model_width)
    outgoing_slots = slot_ids[ordering].reshape(device_count, pair_rows)
    arrived, arrived_slots = (
        lax.all_to_all(outgoing, ("slide", "ctx"), split_axis=0, concat_axis=0, tiled=True),
        lax.all_to_all(outgoing_slots, ("slide", "ctx"), split_axis=0, concat_axis=0, tiled=True),
    )
    placing = jnp.argsort(arrived_slots.reshape(block_rows) % block_rows)
    tokens = arrived.reshape(block_rows, model_width)[placing]
    return layer(tokens, lengths, ln_gain_attn, w_query, w_kv, w_out, ln_gain_mlp, w_up, w_down)


def solution(mesh):
    return jax.shard_map(
        on_device,
        mesh=mesh,
        in_specs=(
            P(("slide", "ctx"), None),
            P(("slide", "ctx"), None),
            P("slide"),
            P(),
            P("slide", None),
            P("slide", None),
            P("slide", None),
            P(),
            P("slide", None),
            P("slide", None),
        ),
        out_specs=P(("slide", "ctx"), None),
        check_vma=False,
    )
```

```python
import functools

import jax
import jax.numpy as jnp
from jax import lax
from jax.experimental import pallas as pl
from jax.experimental.pallas import tpu as pltpu
from jax.sharding import PartitionSpec as P

HEAD_DIM = 64
MESH = pl.DeviceIdType.MESH
bf16, f32 = jnp.bfloat16, jnp.float32

norm_eps = 1e-05
masked_score = -1e30
value_rows = 80
ORDER = [
    (0, 0), (0, 1), (1, 0), (2, 0), (3, 0), (1, 1), (2, 1), (3, 1),
    (6, 0), (5, 0), (6, 1), (4, 0), (7, 0), (4, 1), (5, 1), (7, 1),
]


def layer_norm(rows, gain):
    values32 = rows.astype(f32)
    row_mean = jnp.mean(values32, axis=-1, keepdims=True)
    centred = values32 - row_mean
    row_var = jnp.mean(centred * centred, axis=-1, keepdims=True)
    return (centred * lax.rsqrt(row_var + norm_eps) * gain).astype(bf16)


def dot(left, right):
    return jnp.dot(left, right, preferred_element_type=f32)


def dot_nt(left, right):
    return lax.dot_general(left, right, (((1,), (1,)), ((), ())), preferred_element_type=f32)


def identity(size):
    row = lax.broadcasted_iota(jnp.int32, (size, size), 0)
    column = lax.broadcasted_iota(jnp.int32, (size, size), 1)
    return jnp.where(row == column, 1.0, 0.0).astype(bf16)


def layer_kernel(
    tile_rows, tile_slot, length_ref, gain1, wq, wkv, wo, gain2, wu, wd,
    out,
    outgoing, in_slide, by_ctx, in_block, tok, masks, eye,
    rows, w_a, w_b, w_c, w_vt, q_aug, k_buf, v_buf, bias, scores, top, acc, attended, up_buf, down_acc,
    s_send, s_recv, p_send, p_recv, m_send, m_recv, t_send, t_recv, a_send, a_recv, b_send, b_recv, c_send, c_recv,
):
    block, width = tok.shape
    half = block // 2
    heads = width // HEAD_DIM
    pairs = heads // 2
    hidden = wu.shape[1]
    slide = lax.axis_index("slide")
    ctx = lax.axis_index("ctx")
    z_hi, x, core = lax.div(slide, 8), lax.rem(lax.div(slide, 2), 4), lax.rem(slide, 2)
    y, z_lo = lax.div(ctx, 2), lax.rem(ctx, 2)

    def at_slide(zz, xx, cc):
        return zz * 8 + lax.rem(xx + 4, 4) * 2 + cc

    def at_ctx(yy, zz):
        return lax.rem(yy + 4, 4) * 2 + zz

    y_next = (slide, at_ctx(y + 1, z_lo))
    y_prev = (slide, at_ctx(y - 1, z_lo))
    z_pair = (slide, at_ctx(y, 1 - z_lo))
    x_next = (at_slide(z_hi, x + 1, core), ctx)
    x_prev = (at_slide(z_hi, x - 1, core), ctx)
    zw_pair = (at_slide(1 - z_hi, x, core), at_ctx(y, 1 - z_lo))
    sibling = (at_slide(z_hi, x, 1 - core), ctx)

    slides, ctxs = 16, 8
    slide_peers = [(lax.rem(slide + by, slides), ctx) for by in range(1, slides)]
    ctx_peers = [(slide, lax.rem(ctx + by, ctxs)) for by in range(1, ctxs)]
    barrier = pltpu.get_barrier_semaphore()
    for peer in slide_peers + ctx_peers + [zw_pair]:
        pl.semaphore_signal(barrier, inc=1, device_id=peer, device_id_type=MESH)
    pl.semaphore_wait(barrier, slides + ctxs - 1)

    def shard_of(relation, cc):
        zz = (1 - z_hi) if relation in (3, 4, 5, 7) else z_hi
        step = {0: 0, 1: -1, 2: 1, 3: 0, 4: -1, 5: 1, 6: 2, 7: 2}[relation]
        return at_slide(zz, x + step, cc)

    class Gather:
        def __init__(self, whole, depth, send, recv):
            self.whole, self.depth, self.send, self.recv = whole, depth, send, recv
            self.started = []

        def part(self, relation, cc, side=None):
            at = pl.ds(pl.multiple_of(shard_of(relation, cc) * self.depth, 16), self.depth)
            if side is None:
                return self.whole.at[at, :]
            cut = self.whole.shape[1] // 2
            return self.whole.at[at, pl.ds(side * cut, cut)]

        def handle(self, key, send_slot, slot, peer):
            part = self.part(*key)
            return pltpu.make_async_remote_copy(
                src_ref=part, dst_ref=part, send_sem=self.send.at[send_slot],
                recv_sem=self.recv.at[slot], device_id=peer, device_id_type=MESH,
            )

        def copy(self, key, peer, slot):
            self.handle(key, len(self.started), slot, peer).start()
            self.started.append(key)

        def arrive(self, key, slot):
            self.handle(key, 0, slot, sibling).wait_recv()

        def first(self):
            own = (0, core)
            self.copy(own, x_next, 1)
            self.copy(own, x_prev, 2)
            self.copy(own, zw_pair, 3)
            self.copy(own, sibling, 8)

        def second(self):
            for relation in (1, 2, 3):
                self.arrive((relation, core), relation)
            self.copy((1, core, 0), x_next, 6)
            self.copy((2, core, 1), x_prev, 0)
            self.copy((3, core), x_next, 4)
            self.copy((3, core), x_prev, 5)
            for relation in (1, 2, 3):
                self.copy((relation, core), sibling, 8 + relation)

        def third(self):
            self.arrive((6, core, 0), 6)
            self.arrive((6, core, 1), 0)
            self.copy((6, core), zw_pair, 7)
            self.copy((6, core), sibling, 14)

        def fourth(self):
            for relation in (4, 5, 7):
                self.arrive((relation, core), relation)
                self.copy((relation, core), sibling, 8 + relation)

        def last(self):
            for relation in range(8):
                self.arrive((relation, 1 - core), 8 + relation)

        def sent(self):
            for index, key in enumerate(self.started):
                self.handle(key, index, 0, sibling).wait_send()

    gather_a = Gather(w_a, wq.shape[0], a_send, a_recv)
    gather_b = Gather(w_b, wu.shape[0], b_send, b_recv)
    gather_c = Gather(w_c, wd.shape[0], c_send, c_recv)

    own48 = pl.ds(pl.multiple_of(slide * wq.shape[0], 16), wq.shape[0])
    w_a[own48, 0:width] = wq[...]
    w_a[own48, width:] = wkv[...]
    gather_a.first()

    def grid(shape, dim):
        return lax.broadcasted_iota(jnp.int32, shape, dim)

    slots = tile_slot[...]
    devices = slides * ctxs
    share = block // devices
    owned = jnp.where((slots >> 9) == grid((devices, block), 0), 1.0, 0.0)
    earlier = jnp.where(grid((block, block), 0) < grid((block, block), 1), 1.0, 0.0).astype(bf16)
    ahead = dot(owned.astype(bf16), earlier)
    first_row = (grid((devices, block), 0) * share).astype(f32)
    target = jnp.sum(owned * (first_row + ahead), axis=0, keepdims=True)
    sorting = jnp.where(grid((block, block), 0).astype(f32) == target, 1.0, 0.0).astype(bf16)
    lane = grid((128, block), 0)
    digits = jnp.where(lane == 0, (slots >> 6) & 63, jnp.where(lane == 1, slots & 63, 0))
    outgoing[:, 0:width] = dot(sorting, tile_rows[...]).astype(bf16)
    outgoing[:, width:] = dot_nt(sorting, digits.astype(f32).astype(bf16)).astype(bf16)

    def pieces(buffer, index, depth):
        return buffer.at[pl.ds(pl.multiple_of(index * depth, 16), depth), :]

    def exchange(source, target, depth, me, count, peers, send, recv):
        def handle(by, peer):
            return pltpu.make_async_remote_copy(
                src_ref=pieces(source, lax.rem(me + by, count), depth),
                dst_ref=pieces(target, me, depth), send_sem=send.at[by],
                recv_sem=recv.at[by], device_id=peer, device_id_type=MESH,
            )

        def incoming(by, peer):
            part = pieces(target, lax.rem(me + count - by, count), depth)
            return pltpu.make_async_remote_copy(
                src_ref=part, dst_ref=part, send_sem=send.at[by],
                recv_sem=recv.at[by], device_id=peer, device_id_type=MESH,
            )

        def start():
            for by in range(1, count):
                handle(by, peers[by - 1]).start()
            at = pl.ds(pl.multiple_of(me * depth, 16), depth)
            target[at, :] = source[at, :]

        def arrive():
            for by in range(1, count):
                incoming(by, peers[by - 1]).wait_recv()

        def sent():
            for by in range(1, count):
                handle(by, peers[by - 1]).wait_send()

        return start, arrive, sent

    slide_rows = block // slides
    ctx_rows = block // ctxs
    to_slides = exchange(outgoing, in_slide, slide_rows, slide, slides, slide_peers, s_send, s_recv)
    to_blocks = exchange(by_ctx, in_block, ctx_rows, ctx, ctxs, ctx_peers, p_send, p_recv)
    to_slides[0]()

    w_b[own48, 0:width] = wo[...]
    w_b[own48, width:] = wu[...]
    own192 = pl.ds(pl.multiple_of(slide * wd.shape[0], 16), wd.shape[0])
    w_c[own192, :] = wd[...]
    eye[...] = identity(width)
    q_aug[...] = jnp.zeros(q_aug.shape, bf16)
    q_aug[:, 128:144, :] = jnp.where(grid((pairs, 16, 2 * block), 1) == 0, 1.0, 0.0).astype(bf16)
    v_buf[:, 64:80, :] = jnp.where(grid((heads, 16, block), 1) == 0, 1.0, 0.0).astype(bf16)
    top[...] = jnp.full(top.shape, masked_score, f32)
    acc[...] = jnp.zeros(acc.shape, f32)
    gather_a.second()

    to_slides[1]()
    wanted = grid((block, block), 0)
    wanted = ((wanted >> 2) & 15) * slide_rows + (wanted >> 6) * share + (wanted & 3)
    turning = jnp.where(grid((block, block), 1) == wanted, 1.0, 0.0).astype(bf16)
    by_ctx[...] = dot(turning, in_slide[...]).astype(bf16)
    to_blocks[0]()

    place = {key: index for index, key in enumerate(ORDER)}

    def chunk(relation, side):
        return rows.at[pl.ds(place[relation, side] * half, half), :]

    token_sends = []

    def rows_handle(source, target, send_slot, peer):
        return pltpu.make_async_remote_copy(
            src_ref=chunk(*source), dst_ref=chunk(*target), send_sem=t_send.at[send_slot],
            recv_sem=t_recv.at[place[target]], device_id=peer, device_id_type=MESH,
        )

    def pass_rows(source, relation, side, peer):
        rows_handle(source, (relation, side), len(token_sends), peer).start()
        token_sends.append(source)

    def rows_here(relation, side):
        rows_handle((relation, side), (relation, side), 0, sibling).wait_recv()

    for side in range(2):
        part = slice(side * half, (side + 1) * half)
        rows[part, :] = layer_norm(in_slide[part, 0:width], gain1[...])
        pass_rows((0, side), 1, side, y_next)
        pass_rows((0, side), 2, side, y_prev)
        pass_rows((0, side), 3, side, z_pair)

    def positions(buffer):
        weight = grid((8, 128), 1)
        weight = jnp.where(weight == 0, 64.0, jnp.where(weight == 1, 1.0, 0.0)).astype(bf16)
        return dot_nt(weight, buffer[:, width:])

    length = length_ref[0]
    masked = jnp.where(positions(in_slide) >= length.astype(f32), masked_score, 0.0)
    masks[ctx, 0] = masked[:, 0:half]
    masks[ctx, 1] = masked[:, half:]

    def mask_handle(by, owner):
        return pltpu.make_async_remote_copy(
            src_ref=masks.at[owner], dst_ref=masks.at[owner], send_sem=m_send.at[by],
            recv_sem=m_recv.at[by], device_id=ctx_peers[by - 1], device_id_type=MESH,
        )

    for by in range(1, ctxs):
        mask_handle(by, ctx).start()

    gather_a.third()
    gather_a.fourth()
    gather_b.first()
    gather_a.last()
    w_vt[...] = dot_nt(eye[...], w_a[:, 2 * width :]).astype(bf16)

    def project(step):
        here = rows[pl.ds(pl.multiple_of(step * block, block), block), :]
        k_buf[...] = dot(here, w_a[:, width : 2 * width]).astype(bf16)
        values_t = dot_nt(w_vt[...], here).astype(bf16)
        for head in range(heads):
            v_buf[head, 0:64, :] = values_t[head * 64 : head * 64 + 64, :]

    project(0)

    to_blocks[1]()
    at_row = positions(in_block)[0:1] - (ctx * block).astype(f32)
    placing = jnp.where(grid((block, block), 0).astype(f32) == at_row, 1.0, 0.0).astype(bf16)
    tok[...] = dot(placing, in_block[:, 0:width]).astype(bf16)

    scale = HEAD_DIM ** (-0.5) * 1.4426950408889634
    queries = (dot(layer_norm(tok[...], gain1[...]), w_a[:, 0:width]) * scale).astype(bf16)
    queries_t = dot_nt(eye[...], queries).astype(bf16)
    for head in range(heads):
        pair, at = head // 2, head % 2
        q_aug[pair, at * 64 : at * 64 + 64, at * block : (at + 1) * block] = queries_t[
            head * 64 : head * 64 + 64, :
        ]

    for by in range(1, ctxs):
        mask_handle(by, lax.rem(ctx + ctxs - by, ctxs)).wait_recv()

    def owner(relation):
        step = {0: 0, 1: -1, 2: 1, 3: 0, 4: -1, 5: 1, 6: 2, 7: 2}[relation]
        zz = (1 - z_lo) if relation in (3, 4, 5, 7) else z_lo
        return at_ctx(y + step, zz)

    def attend(first, first_side, second, second_side):
        here = jnp.concatenate([masks[first, first_side], masks[second, second_side]], axis=1)
        here = jnp.concatenate([here, jnp.zeros((120, block), f32)], axis=0).astype(bf16)
        bias[...] = dot_nt(eye[0:block, 0:block], here).astype(bf16)

        def score(pair, slot):
            keys = k_buf[:, pl.ds(pl.multiple_of(pair * 128, 128), 128)]
            scores[slot] = dot(jnp.concatenate([keys, bias[...]], axis=1), q_aug[pair])

        def soften(pair, slot):
            before = top[pair]
            now = jnp.maximum(before, jnp.max(scores[slot], axis=0, keepdims=True))
            factor = jnp.exp2(before - now)
            top[pair] = now
            for side in range(2):
                span = slice(side * block, (side + 1) * block)
                weights = jnp.exp2(scores[slot, :, span] - now[:, span]).astype(bf16)
                head = 2 * pair + side
                acc[head] = acc[head] * factor[:, span] + dot(v_buf[head], weights)

        score(0, 0)

        def two(index, _):
            score(2 * index + 1, 1)
            soften(2 * index, 0)
            score(jnp.minimum(2 * index + 2, pairs - 1), 0)
            soften(2 * index + 1, 1)
            return 0

        lax.fori_loop(0, pairs // 2, two, 0)

    steps = len(ORDER) // 2
    firsts = [owner(ORDER[2 * step][0]) for step in range(steps)]
    seconds = [owner(ORDER[2 * step + 1][0]) for step in range(steps)]
    first_sides = [ORDER[2 * step][1] for step in range(steps)]
    second_sides = [ORDER[2 * step + 1][1] for step in range(steps)]

    def pick(options, step):
        chosen = options[0]
        for index in range(1, len(options)):
            chosen = jnp.where(step == index, options[index], chosen)
        return chosen

    def turn(step, _):
        @pl.when(step == 1)
        def _():
            for relation in (1, 2, 3):
                rows_here(relation, 0)
            pass_rows((1, 0), 6, 0, y_next)
            pass_rows((3, 0), 5, 0, y_prev)
            pass_rows((3, 0), 4, 0, y_next)

        @pl.when(step == 2)
        def _():
            for relation in (1, 2, 3):
                rows_here(relation, 1)
            pass_rows((3, 1), 4, 1, y_next)
            pass_rows((2, 1), 6, 1, y_prev)
            pass_rows((3, 1), 5, 1, y_prev)
            gather_b.second()

        @pl.when(step == 3)
        def _():
            gather_b.third()
            gather_c.first()

        @pl.when(step == 4)
        def _():
            rows_here(6, 0)
            pass_rows((6, 0), 7, 0, z_pair)
            rows_here(5, 0)
            gather_b.fourth()

        @pl.when(step == 5)
        def _():
            rows_here(6, 1)
            pass_rows((6, 1), 7, 1, z_pair)
            rows_here(4, 0)
            gather_c.second()

        @pl.when(step == 6)
        def _():
            rows_here(7, 0)
            rows_here(4, 1)
            gather_c.third()

        @pl.when(step == 7)
        def _():
            rows_here(5, 1)
            rows_here(7, 1)
            gather_c.fourth()

        @pl.when(step > 0)
        def _():
            project(step)

        attend(
            pick(firsts, step), pick(first_sides, step), pick(seconds, step), pick(second_sides, step)
        )
        return 0

    lax.fori_loop(0, steps, turn, 0)

    gather_b.last()
    for head in range(heads):
        done = acc[head]
        attended[head * 64 : head * 64 + 64, :] = (done[0:64] / done[64:65]).astype(bf16)
    turned = dot_nt(eye[0:block, 0:block], attended[...]).astype(bf16)
    mid = (tok[...].astype(f32) + dot(turned, w_b[:, 0:width])).astype(bf16)
    for index, source in enumerate(token_sends):
        rows_handle(source, source, index, sibling).wait_send()
    rows[0:block, :] = layer_norm(mid, gain2[...])
    gather_c.last()
    down_acc[...] = mid.astype(f32)

    tile = up_buf.shape[2]
    tiles = hidden // tile

    def up(index, slot):
        at = pl.ds(pl.multiple_of(width + index * tile, 128), tile)
        up_buf[slot] = dot(rows[0:block, :], w_b[:, at])

    def down(index, slot):
        active = jax.nn.gelu(up_buf[slot], approximate=True).astype(bf16)
        down_acc[...] += dot(active, w_c[pl.ds(pl.multiple_of(index * tile, tile), tile), :])

    up(0, 0)

    def two_tiles(index, _):
        up(2 * index + 1, 1)
        down(2 * index, 0)
        up(jnp.minimum(2 * index + 2, tiles - 1), 0)
        down(2 * index + 1, 1)
        return 0

    lax.fori_loop(0, tiles // 2, two_tiles, 0)
    at = ctx * block + lax.broadcasted_iota(jnp.int32, (block, width), 0)
    out[...] = jnp.where(at < length, down_acc[...], 0.0).astype(bf16)

    to_slides[2]()
    to_blocks[2]()
    for by in range(1, ctxs):
        mask_handle(by, ctx).wait_send()
    for gather in (gather_a, gather_b, gather_c):
        gather.sent()


def on_device(
    tile_rows, tile_slot, lengths, ln_gain_attn, w_query, w_kv, w_out, ln_gain_mlp, w_up, w_down
):
    block, width = tile_rows.shape
    heads = width // HEAD_DIM
    hidden = w_up.shape[1]
    vmem = pl.BlockSpec(memory_space=pltpu.VMEM)
    dma = pltpu.SemaphoreType.DMA
    return pl.pallas_call(
        layer_kernel,
        out_shape=jax.ShapeDtypeStruct((block, width), bf16),
        in_specs=[vmem, vmem, pl.BlockSpec(memory_space=pltpu.SMEM)] + [vmem] * 7,
        out_specs=vmem,
        scratch_shapes=[
            pltpu.VMEM((block, width + 128), bf16),
            pltpu.VMEM((block, width + 128), bf16),
            pltpu.VMEM((block, width + 128), bf16),
            pltpu.VMEM((block, width + 128), bf16),
            pltpu.VMEM((block, width), bf16),
            pltpu.VMEM((8, 2, 8, block // 2), f32),
            pltpu.VMEM((width, width), bf16),
            pltpu.VMEM((8 * block, width), bf16),
            pltpu.VMEM((width, 3 * width), bf16),
            pltpu.VMEM((width, width + hidden), bf16),
            pltpu.VMEM((hidden, width), bf16),
            pltpu.VMEM((width, width), bf16),
            pltpu.VMEM((heads // 2, 256, 2 * block), bf16),
            pltpu.VMEM((block, width), bf16),
            pltpu.VMEM((heads, value_rows, block), bf16),
            pltpu.VMEM((block, 128), bf16),
            pltpu.VMEM((2, block, 2 * block), f32),
            pltpu.VMEM((heads // 2, 1, 2 * block), f32),
            pltpu.VMEM((heads, value_rows, block), f32),
            pltpu.VMEM((width, block), bf16),
            pltpu.VMEM((2, block, 512), f32),
            pltpu.VMEM((block, width), f32),
            dma((16,)), dma((16,)),
            dma((8,)), dma((8,)),
            dma((8,)), dma((8,)),
            dma((14,)), dma((16,)),
            dma((16,)), dma((16,)),
            dma((16,)), dma((16,)),
            dma((16,)), dma((16,)),
        ],
        compiler_params=pltpu.CompilerParams(
            collective_id=0, has_side_effects=True, vmem_limit_bytes=60 * 2**20
        ),
        name="layer",
    )(
        tile_rows, tile_slot, lengths, ln_gain_attn.reshape(1, width), w_query, w_kv, w_out,
        ln_gain_mlp.reshape(1, width), w_up, w_down,
    )


def solution(mesh):
    return jax.shard_map(
        on_device,
        mesh=mesh,
        in_specs=(
            P(("slide", "ctx"), None),
            P(("slide", "ctx"), None),
            P("slide"),
            P(),
            P("slide", None),
            P("slide", None),
            P("slide", None),
            P(),
            P("slide", None),
            P("slide", None),
        ),
        out_specs=P(("slide", "ctx"), None),
        check_vma=False,
    )
```

```python
import functools

import jax
import jax.numpy as jnp
from jax import lax
from jax.experimental import pallas as pl
from jax.experimental.pallas import tpu as pltpu
from jax.sharding import PartitionSpec as P

HEAD_DIM = 64
MESH = pl.DeviceIdType.MESH
bf16, f32 = jnp.bfloat16, jnp.float32

norm_eps = 1e-05
masked_score = -1e30
value_rows = 80
ORDER = [
    (0, 0), (0, 1), (4, 0), (4, 1), (1, 0), (2, 1), (5, 0), (6, 1),
    (1, 1), (2, 0), (5, 1), (6, 0), (3, 0), (3, 1), (7, 0), (7, 1),
]


def layer_norm(rows, gain):
    values32 = rows.astype(f32)
    row_mean = jnp.mean(values32, axis=-1, keepdims=True)
    centred = values32 - row_mean
    row_var = jnp.mean(centred * centred, axis=-1, keepdims=True)
    return (centred * lax.rsqrt(row_var + norm_eps) * gain).astype(bf16)


def dot(left, right):
    return jnp.dot(left, right, preferred_element_type=f32)


def dot_nt(left, right):
    return lax.dot_general(left, right, (((1,), (1,)), ((), ())), preferred_element_type=f32)


def identity(size):
    row = lax.broadcasted_iota(jnp.int32, (size, size), 0)
    column = lax.broadcasted_iota(jnp.int32, (size, size), 1)
    return jnp.where(row == column, 1.0, 0.0).astype(bf16)


def layer_kernel(
    tile_rows, tile_slot, length_ref, gain1, wq, wkv, wo, gain2, wu, wd,
    out,
    outgoing, in_slide, by_ctx, finished, landed, lengths, masks, eye,
    rows, w_a, w_b, w_c, w_vt, q_aug, k_buf, v_buf, bias, scores, top, acc, attended, up_buf, down_acc,
    s_send, s_recv, f_send, f_recv, m_send, m_recv, l_sem, t_send, t_recv, a_send, a_recv, b_send, b_recv, c_send, c_recv,
):
    block, width = tile_rows.shape
    half = block // 2
    heads = width // HEAD_DIM
    pairs = heads // 2
    hidden = wu.shape[1]
    slide = lax.axis_index("slide")
    ctx = lax.axis_index("ctx")
    z_hi, x, core = lax.div(slide, 8), lax.rem(lax.div(slide, 2), 4), lax.rem(slide, 2)
    y, z_lo = lax.div(ctx, 2), lax.rem(ctx, 2)

    def at_slide(zz, xx, cc):
        return zz * 8 + lax.rem(xx + 4, 4) * 2 + cc

    def at_ctx(yy, zz):
        return lax.rem(yy + 4, 4) * 2 + zz

    slides, ctxs = 16, 8
    y_next = (slide, at_ctx(y + 1, z_lo))
    y_prev = (slide, at_ctx(y - 1, z_lo))
    x_next = (at_slide(z_hi, x + 1, core), ctx)
    x_prev = (at_slide(z_hi, x - 1, core), ctx)
    zw_pair = (at_slide(1 - z_hi, x, core), at_ctx(y, 1 - z_lo))
    sibling = (at_slide(z_hi, x, 1 - core), ctx)

    work = at_slide(z_hi, x, z_lo)
    member = y * 2 + core

    def works_on(index):
        return (
            at_slide(lax.div(index, 8), lax.rem(lax.div(index, 2), 4), core),
            at_ctx(y, lax.rem(index, 2)),
        )

    def at_member(index):
        return (at_slide(z_hi, x, lax.rem(index, 2)), at_ctx(lax.div(index, 2), z_lo))

    work_peers = [works_on(lax.rem(work + by, slides)) for by in range(1, slides)]
    members = [at_member(lax.rem(member + by, ctxs)) for by in range(1, ctxs)]
    near = [
        (at_slide(z_hi, x, lax.rem(core + c, 2)), at_ctx(y + yy, lax.rem(z_lo + zz, 2)))
        for c in range(2) for yy in range(4) for zz in range(2) if (c, yy) != (0, 0)
    ]
    barrier = pltpu.get_barrier_semaphore()
    for peer in work_peers + near:
        pl.semaphore_signal(barrier, inc=1, device_id=peer, device_id_type=MESH)
    pl.semaphore_wait(barrier, len(work_peers) + len(near))

    def shard_of(relation, cc):
        zz = (1 - z_hi) if relation in (3, 4, 5, 7) else z_hi
        step = {0: 0, 1: -1, 2: 1, 3: 0, 4: -1, 5: 1, 6: 2, 7: 2}[relation]
        return at_slide(zz, x + step, cc)

    class Gather:
        def __init__(self, whole, depth, send, recv):
            self.whole, self.depth, self.send, self.recv = whole, depth, send, recv
            self.started = []

        def part(self, relation, cc, side=None):
            at = pl.ds(pl.multiple_of(shard_of(relation, cc) * self.depth, 16), self.depth)
            if side is None:
                return self.whole.at[at, :]
            cut = self.whole.shape[1] // 2
            return self.whole.at[at, pl.ds(side * cut, cut)]

        def handle(self, key, send_slot, slot, peer):
            part = self.part(*key)
            return pltpu.make_async_remote_copy(
                src_ref=part, dst_ref=part, send_sem=self.send.at[send_slot],
                recv_sem=self.recv.at[slot], device_id=peer, device_id_type=MESH,
            )

        def copy(self, key, peer, slot):
            self.handle(key, len(self.started), slot, peer).start()
            self.started.append(key)

        def arrive(self, key, slot):
            self.handle(key, 0, slot, sibling).wait_recv()

        def first(self):
            own = (0, core)
            self.copy(own, x_next, 1)
            self.copy(own, x_prev, 2)
            self.copy(own, zw_pair, 3)
            self.copy(own, sibling, 8)

        def second(self):
            for relation in (1, 2, 3):
                self.arrive((relation, core), relation)
            self.copy((1, core, 0), x_next, 6)
            self.copy((2, core, 1), x_prev, 0)
            self.copy((3, core), x_next, 4)
            self.copy((3, core), x_prev, 5)
            for relation in (1, 2, 3):
                self.copy((relation, core), sibling, 8 + relation)

        def third(self):
            self.arrive((6, core, 0), 6)
            self.arrive((6, core, 1), 0)
            self.copy((6, core), zw_pair, 7)
            self.copy((6, core), sibling, 14)

        def fourth(self):
            for relation in (4, 5, 7):
                self.arrive((relation, core), relation)
                self.copy((relation, core), sibling, 8 + relation)

        def last(self):
            for relation in range(8):
                self.arrive((relation, 1 - core), 8 + relation)

        def sent(self):
            for index, key in enumerate(self.started):
                self.handle(key, index, 0, sibling).wait_send()

    gather_a = Gather(w_a, wq.shape[0], a_send, a_recv)
    gather_b = Gather(w_b, wu.shape[0], b_send, b_recv)
    gather_c = Gather(w_c, wd.shape[0], c_send, c_recv)

    own48 = pl.ds(pl.multiple_of(slide * wq.shape[0], 16), wq.shape[0])
    w_a[own48, 0:width] = wq[...]
    w_a[own48, width:] = wkv[...]
    gather_a.first()
    lengths[0] = jnp.full(lengths.shape[1:], length_ref[0], jnp.int32)

    def length_handle():
        return pltpu.make_async_remote_copy(
            src_ref=lengths.at[0], dst_ref=lengths.at[1], send_sem=l_sem.at[0],
            recv_sem=l_sem.at[1], device_id=sibling, device_id_type=MESH,
        )

    length_handle().start()

    def grid(shape, dim):
        return lax.broadcasted_iota(jnp.int32, shape, dim)

    slots = tile_slot[...]
    devices = slides * ctxs
    share = block // devices
    owned = jnp.where((slots >> 9) == grid((devices, block), 0), 1.0, 0.0)
    earlier = jnp.where(grid((block, block), 0) < grid((block, block), 1), 1.0, 0.0).astype(bf16)
    ahead = dot(owned.astype(bf16), earlier)
    first_row = (grid((devices, block), 0) * share).astype(f32)
    target = jnp.sum(owned * (first_row + ahead), axis=0, keepdims=True)
    sorting = jnp.where(grid((block, block), 0).astype(f32) == target, 1.0, 0.0).astype(bf16)
    lane = grid((128, block), 0)
    digits = jnp.where(lane == 0, (slots >> 6) & 63, jnp.where(lane == 1, slots & 63, 0))
    outgoing[:, 0:width] = dot(sorting, tile_rows[...]).astype(bf16)
    outgoing[:, width:] = dot_nt(sorting, digits.astype(f32).astype(bf16)).astype(bf16)

    def pieces(buffer, index, depth):
        return buffer.at[pl.ds(pl.multiple_of(index * depth, 16), depth), :]

    slide_rows = block // slides

    def to_work(by):
        return pltpu.make_async_remote_copy(
            src_ref=pieces(outgoing, lax.rem(work + by, slides), slide_rows),
            dst_ref=pieces(in_slide, work, slide_rows), send_sem=s_send.at[by],
            recv_sem=s_recv.at[by], device_id=work_peers[by - 1], device_id_type=MESH,
        )

    def from_work(by):
        part = pieces(in_slide, lax.rem(work + slides - by, slides), slide_rows)
        return pltpu.make_async_remote_copy(
            src_ref=part, dst_ref=part, send_sem=s_send.at[by],
            recv_sem=s_recv.at[by], device_id=work_peers[by - 1], device_id_type=MESH,
        )

    for by in range(1, slides):
        to_work(by).start()
    own32 = pl.ds(pl.multiple_of(work * slide_rows, 16), slide_rows)
    in_slide[own32, :] = outgoing[own32, :]

    w_b[own48, 0:width] = wo[...]
    w_b[own48, width:] = wu[...]
    own192 = pl.ds(pl.multiple_of(slide * wd.shape[0], 16), wd.shape[0])
    w_c[own192, :] = wd[...]
    eye[...] = identity(width)
    q_aug[...] = jnp.zeros(q_aug.shape, bf16)
    q_aug[:, 128:144, :] = jnp.where(grid((pairs, 16, 2 * block), 1) == 0, 1.0, 0.0).astype(bf16)
    v_buf[:, 64:80, :] = jnp.where(grid((heads, 16, block), 1) == 0, 1.0, 0.0).astype(bf16)
    top[...] = jnp.full(top.shape, masked_score, f32)
    acc[...] = jnp.zeros(acc.shape, f32)
    gather_a.second()

    for by in range(1, slides):
        from_work(by).wait_recv()
    wanted = grid((block, block), 0)
    wanted = ((wanted >> 2) & 15) * slide_rows + (wanted >> 6) * share + (wanted & 3)
    turning = jnp.where(grid((block, block), 1) == wanted, 1.0, 0.0).astype(bf16)
    by_ctx[...] = dot(turning, in_slide[...]).astype(bf16)

    place = {key: index for index, key in enumerate(ORDER)}

    def chunk(relation, side):
        return rows.at[pl.ds(place[relation, side] * half, half), :]

    token_sends = []

    def rows_handle(source, target, send_slot, peer):
        return pltpu.make_async_remote_copy(
            src_ref=chunk(*source), dst_ref=chunk(*target), send_sem=t_send.at[send_slot],
            recv_sem=t_recv.at[place[target]], device_id=peer, device_id_type=MESH,
        )

    def pass_rows(source, relation, side, peer):
        rows_handle(source, (relation, side), len(token_sends), peer).start()
        token_sends.append(source)

    def rows_here(relation, side):
        rows_handle((relation, side), (relation, side), 0, sibling).wait_recv()

    for side in range(2):
        part = slice(side * half, (side + 1) * half)
        rows[part, :] = layer_norm(by_ctx[part, 0:width], gain1[...])
        if side == 0:
            pass_rows((0, 0), 1, 0, y_next)
        else:
            pass_rows((0, 1), 2, 1, y_prev)
            pass_rows((0, 1), 1, 1, y_next)
            pass_rows((0, 0), 2, 0, y_prev)
        pass_rows((0, side), 4, side, sibling)

    def positions(buffer):
        weight = grid((8, 128), 1)
        weight = jnp.where(weight == 0, 64.0, jnp.where(weight == 1, 1.0, 0.0)).astype(bf16)
        return dot_nt(weight, buffer[:, width:])

    length_handle().wait()
    valid = jnp.where(core == z_lo, lengths[0, 0:1, 0:1], lengths[1, 0:1, 0:1]).astype(f32)
    masked = jnp.where(positions(by_ctx) >= valid, masked_score, 0.0)
    masks[member, 0] = masked[:, 0:half]
    masks[member, 1] = masked[:, half:]

    def mask_handle(by, owner):
        return pltpu.make_async_remote_copy(
            src_ref=masks.at[owner], dst_ref=masks.at[owner], send_sem=m_send.at[by],
            recv_sem=m_recv.at[by], device_id=members[by - 1], device_id_type=MESH,
        )

    for by in range(1, ctxs):
        mask_handle(by, member).start()

    gather_a.third()
    gather_a.fourth()
    gather_b.first()
    gather_a.last()
    w_vt[...] = dot_nt(eye[...], w_a[:, 2 * width :]).astype(bf16)

    def project(step):
        here = rows[pl.ds(pl.multiple_of(step * block, block), block), :]
        k_buf[...] = dot(here, w_a[:, width : 2 * width]).astype(bf16)
        values_t = dot_nt(w_vt[...], here).astype(bf16)
        for head in range(heads):
            v_buf[head, 0:64, :] = values_t[head * 64 : head * 64 + 64, :]

    project(0)

    scale = HEAD_DIM ** (-0.5) * 1.4426950408889634
    queries = (dot(rows[0:block, :], w_a[:, 0:width]) * scale).astype(bf16)
    queries_t = dot_nt(eye[...], queries).astype(bf16)
    for head in range(heads):
        pair, at = head // 2, head % 2
        q_aug[pair, at * 64 : at * 64 + 64, at * block : (at + 1) * block] = queries_t[
            head * 64 : head * 64 + 64, :
        ]

    for by in range(1, ctxs):
        mask_handle(by, lax.rem(member + ctxs - by, ctxs)).wait_recv()

    def owner(relation):
        yy = lax.rem(y + {0: 0, 1: 3, 2: 1, 3: 2}[relation % 4], 4)
        return yy * 2 + ((1 - core) if relation >= 4 else core)

    def attend(first, first_side, second, second_side):
        here = jnp.concatenate([masks[first, first_side], masks[second, second_side]], axis=1)
        here = jnp.concatenate([here, jnp.zeros((120, block), f32)], axis=0).astype(bf16)
        bias[...] = dot_nt(eye[0:block, 0:block], here).astype(bf16)

        def score(pair, slot):
            keys = k_buf[:, pl.ds(pl.multiple_of(pair * 128, 128), 128)]
            scores[slot] = dot(jnp.concatenate([keys, bias[...]], axis=1), q_aug[pair])

        def soften(pair, slot):
            before = top[pair]
            now = jnp.maximum(before, jnp.max(scores[slot], axis=0, keepdims=True))
            factor = jnp.exp2(before - now)
            top[pair] = now
            for side in range(2):
                span = slice(side * block, (side + 1) * block)
                weights = jnp.exp2(scores[slot, :, span] - now[:, span]).astype(bf16)
                head = 2 * pair + side
                acc[head] = acc[head] * factor[:, span] + dot(v_buf[head], weights)

        score(0, 0)

        def two(index, _):
            score(2 * index + 1, 1)
            soften(2 * index, 0)
            score(jnp.minimum(2 * index + 2, pairs - 1), 0)
            soften(2 * index + 1, 1)
            return 0

        lax.fori_loop(0, pairs // 2, two, 0)

    steps = len(ORDER) // 2
    firsts = [owner(ORDER[2 * step][0]) for step in range(steps)]
    seconds = [owner(ORDER[2 * step + 1][0]) for step in range(steps)]
    first_sides = [ORDER[2 * step][1] for step in range(steps)]
    second_sides = [ORDER[2 * step + 1][1] for step in range(steps)]

    def pick(options, step):
        chosen = options[0]
        for index in range(1, len(options)):
            chosen = jnp.where(step == index, options[index], chosen)
        return chosen

    def turn(step, _):
        @pl.when(step == 1)
        def _():
            rows_here(4, 0)
            rows_here(4, 1)

        @pl.when(step == 2)
        def _():
            rows_here(1, 0)
            pass_rows((1, 0), 3, 0, y_next)
            pass_rows((1, 0), 5, 0, sibling)
            rows_here(2, 1)
            pass_rows((2, 1), 3, 1, y_prev)
            pass_rows((2, 1), 6, 1, sibling)
            gather_b.second()

        @pl.when(step == 3)
        def _():
            rows_here(5, 0)
            rows_here(6, 1)
            gather_b.third()
            gather_c.first()

        @pl.when(step == 4)
        def _():
            rows_here(1, 1)
            pass_rows((1, 1), 5, 1, sibling)
            rows_here(2, 0)
            pass_rows((2, 0), 6, 0, sibling)
            gather_b.fourth()

        @pl.when(step == 5)
        def _():
            rows_here(5, 1)
            rows_here(6, 0)
            gather_c.second()

        @pl.when(step == 6)
        def _():
            rows_here(3, 0)
            pass_rows((3, 0), 7, 0, sibling)
            rows_here(3, 1)
            pass_rows((3, 1), 7, 1, sibling)
            gather_c.third()

        @pl.when(step == 7)
        def _():
            rows_here(7, 0)
            rows_here(7, 1)
            gather_c.fourth()

        @pl.when(step > 0)
        def _():
            project(step)

        attend(
            pick(firsts, step), pick(first_sides, step), pick(seconds, step), pick(second_sides, step)
        )
        return 0

    lax.fori_loop(0, steps, turn, 0)

    gather_b.last()
    for head in range(heads):
        done = acc[head]
        attended[head * 64 : head * 64 + 64, :] = (done[0:64] / done[64:65]).astype(bf16)
    turned = dot_nt(eye[0:block, 0:block], attended[...]).astype(bf16)
    mid = (by_ctx[:, 0:width].astype(f32) + dot(turned, w_b[:, 0:width])).astype(bf16)
    for index, source in enumerate(token_sends):
        rows_handle(source, source, index, sibling).wait_send()
    rows[0:block, :] = layer_norm(mid, gain2[...])
    down_acc[...] = mid.astype(f32)
    finished[:, width:] = by_ctx[:, width:]
    gather_c.last()

    tile = up_buf.shape[2]
    tiles = hidden // tile
    part_rows = block // 4
    ctx_rows = block // ctxs

    def send_home(target_ctx):
        return pltpu.make_async_remote_copy(
            src_ref=pieces(finished, target_ctx, ctx_rows), dst_ref=pieces(landed, member, ctx_rows),
            send_sem=f_send.at[target_ctx], recv_sem=f_recv.at[member],
            device_id=(at_slide(z_hi, x, z_lo), target_ctx), device_id_type=MESH,
        )

    def from_member(index):
        part = pieces(landed, index, ctx_rows)
        return pltpu.make_async_remote_copy(
            src_ref=part, dst_ref=part, send_sem=f_send.at[index], recv_sem=f_recv.at[index],
            device_id=sibling, device_id_type=MESH,
        )

    stays = core == z_lo

    def piece(index, _):
        yy = lax.rem(y + pick([2, 1, 3, 0], index), 4)
        here = pl.ds(pl.multiple_of(yy * part_rows, part_rows), part_rows)

        def up(at, slot):
            span = pl.ds(pl.multiple_of(width + at * tile, 128), tile)
            up_buf[slot] = dot(rows[here, :], w_b[:, span])

        def down(at, slot):
            active = jax.nn.gelu(up_buf[slot], approximate=True).astype(bf16)
            span = pl.ds(pl.multiple_of(at * tile, tile), tile)
            down_acc[here, :] += dot(active, w_c[span, :])

        up(0, 0)

        def two_tiles(at, _):
            up(2 * at + 1, 1)
            down(2 * at, 0)
            up(jnp.minimum(2 * at + 2, tiles - 1), 0)
            down(2 * at + 1, 1)
            return 0

        lax.fori_loop(0, tiles // 2, two_tiles, 0)
        finished[here, 0:width] = down_acc[here, :].astype(bf16)
        for zz in range(2):
            target = yy * 2 + zz
            home = stays & (yy == y) & (z_lo == zz)

            @pl.when(jnp.logical_not(home))
            def _():
                send_home(target).start()

            @pl.when(home)
            def _():
                at = pl.ds(pl.multiple_of(member * ctx_rows, 16), ctx_rows)
                landed[at, :] = finished[pl.ds(pl.multiple_of(target * ctx_rows, 16), ctx_rows), :]

        return 0

    lax.fori_loop(0, 4, piece, 0)

    for index in range(ctxs):
        @pl.when(jnp.logical_not(stays & (member == index)))
        def _():
            from_member(index).wait_recv()

    at_row = positions(landed)[0:1] - (ctx * block).astype(f32)
    placing = jnp.where(grid((block, block), 0).astype(f32) == at_row, 1.0, 0.0).astype(bf16)
    at = ctx * block + grid((block, width), 0)
    out[...] = jnp.where(at < length_ref[0], dot(placing, landed[:, 0:width]), 0.0).astype(bf16)

    for index in range(ctxs):
        @pl.when(jnp.logical_not(stays & (ctx == index)))
        def _():
            send_home(index).wait_send()

    for by in range(1, slides):
        to_work(by).wait_send()
    for by in range(1, ctxs):
        mask_handle(by, member).wait_send()
    for gather in (gather_a, gather_b, gather_c):
        gather.sent()


def on_device(
    tile_rows, tile_slot, lengths, ln_gain_attn, w_query, w_kv, w_out, ln_gain_mlp, w_up, w_down
):
    block, width = tile_rows.shape
    heads = width // HEAD_DIM
    hidden = w_up.shape[1]
    vmem = pl.BlockSpec(memory_space=pltpu.VMEM)
    dma = pltpu.SemaphoreType.DMA
    return pl.pallas_call(
        layer_kernel,
        out_shape=jax.ShapeDtypeStruct((block, width), bf16),
        in_specs=[vmem, vmem, pl.BlockSpec(memory_space=pltpu.SMEM)] + [vmem] * 7,
        out_specs=vmem,
        scratch_shapes=[
            pltpu.VMEM((block, width + 128), bf16),
            pltpu.VMEM((block, width + 128), bf16),
            pltpu.VMEM((block, width + 128), bf16),
            pltpu.VMEM((block, width + 128), bf16),
            pltpu.VMEM((block, width + 128), bf16),
            pltpu.VMEM((2, 8, 128), jnp.int32),
            pltpu.VMEM((8, 2, 8, block // 2), f32),
            pltpu.VMEM((width, width), bf16),
            pltpu.VMEM((8 * block, width), bf16),
            pltpu.VMEM((width, 3 * width), bf16),
            pltpu.VMEM((width, width + hidden), bf16),
            pltpu.VMEM((hidden, width), bf16),
            pltpu.VMEM((width, width), bf16),
            pltpu.VMEM((heads // 2, 256, 2 * block), bf16),
            pltpu.VMEM((block, width), bf16),
            pltpu.VMEM((heads, value_rows, block), bf16),
            pltpu.VMEM((block, 128), bf16),
            pltpu.VMEM((2, block, 2 * block), f32),
            pltpu.VMEM((heads // 2, 1, 2 * block), f32),
            pltpu.VMEM((heads, value_rows, block), f32),
            pltpu.VMEM((width, block), bf16),
            pltpu.VMEM((2, block // 4, 512), f32),
            pltpu.VMEM((block, width), f32),
            dma((16,)), dma((16,)),
            dma((8,)), dma((8,)),
            dma((8,)), dma((8,)),
            dma((2,)),
            dma((14,)), dma((16,)),
            dma((16,)), dma((16,)),
            dma((16,)), dma((16,)),
            dma((16,)), dma((16,)),
        ],
        compiler_params=pltpu.CompilerParams(
            collective_id=0, has_side_effects=True, vmem_limit_bytes=60 * 2**20
        ),
        name="layer",
    )(
        tile_rows, tile_slot, lengths, ln_gain_attn.reshape(1, width), w_query, w_kv, w_out,
        ln_gain_mlp.reshape(1, width), w_up, w_down,
    )


def solution(mesh):
    return jax.shard_map(
        on_device,
        mesh=mesh,
        in_specs=(
            P(("slide", "ctx"), None),
            P(("slide", "ctx"), None),
            P("slide"),
            P(),
            P("slide", None),
            P("slide", None),
            P("slide", None),
            P(),
            P("slide", None),
            P("slide", None),
        ),
        out_specs=P(("slide", "ctx"), None),
        check_vma=False,
    )
```

```python
import functools

import jax
import jax.numpy as jnp
from jax import lax
from jax.experimental import pallas as pl
from jax.experimental.pallas import tpu as pltpu
from jax.sharding import PartitionSpec as P

HEAD_DIM = 64
MESH = pl.DeviceIdType.MESH
bf16, f32 = jnp.bfloat16, jnp.float32

norm_eps = 1e-05
masked_score = -1e30
value_rows = 80
ORDER = [
    (0, 0), (0, 1), (4, 0), (4, 1), (1, 0), (2, 1), (5, 0), (6, 1),
    (1, 1), (2, 0), (5, 1), (6, 0), (3, 0), (3, 1), (7, 0), (7, 1),
]


def layer_norm(rows, gain):
    values32 = rows.astype(f32)
    row_mean = jnp.mean(values32, axis=-1, keepdims=True)
    centred = values32 - row_mean
    row_var = jnp.mean(centred * centred, axis=-1, keepdims=True)
    return (centred * lax.rsqrt(row_var + norm_eps) * gain).astype(bf16)


def dot(left, right):
    return jnp.dot(left, right, preferred_element_type=f32)


def dot_nt(left, right):
    return lax.dot_general(left, right, (((1,), (1,)), ((), ())), preferred_element_type=f32)


def identity(size):
    row = lax.broadcasted_iota(jnp.int32, (size, size), 0)
    column = lax.broadcasted_iota(jnp.int32, (size, size), 1)
    return jnp.where(row == column, 1.0, 0.0).astype(bf16)


def layer_kernel(
    tile_rows, tile_slot, length_ref, gain1, wq, wkv, wo, gain2, wu, wd,
    out,
    outgoing, in_slide, by_ctx, finished, landed, lengths, masks, eye,
    rows, w_a, w_b, w_c, w_vt, q_aug, k_even, k_odd, v_even, v_odd, bias_even, bias_odd, scores, top, acc, attended, up_buf, down_acc,
    s_send, s_recv, f_send, f_recv, m_send, m_recv, l_sem, t_send, t_recv, a_send, a_recv, b_send, b_recv, c_send, c_recv,
):
    block, width = tile_rows.shape
    half = block // 2
    heads = width // HEAD_DIM
    pairs = heads // 2
    hidden = wu.shape[1]
    slide = lax.axis_index("slide")
    ctx = lax.axis_index("ctx")
    z_hi, x, core = lax.div(slide, 8), lax.rem(lax.div(slide, 2), 4), lax.rem(slide, 2)
    y, z_lo = lax.div(ctx, 2), lax.rem(ctx, 2)

    def at_slide(zz, xx, cc):
        return zz * 8 + lax.rem(xx + 4, 4) * 2 + cc

    def at_ctx(yy, zz):
        return lax.rem(yy + 4, 4) * 2 + zz

    slides, ctxs = 16, 8
    y_next = (slide, at_ctx(y + 1, z_lo))
    y_prev = (slide, at_ctx(y - 1, z_lo))
    x_next = (at_slide(z_hi, x + 1, core), ctx)
    x_prev = (at_slide(z_hi, x - 1, core), ctx)
    zw_pair = (at_slide(1 - z_hi, x, core), at_ctx(y, 1 - z_lo))
    sibling = (at_slide(z_hi, x, 1 - core), ctx)

    work = at_slide(z_hi, x, z_lo)
    member = y * 2 + core

    def works_on(index):
        return (
            at_slide(lax.div(index, 8), lax.rem(lax.div(index, 2), 4), core),
            at_ctx(y, lax.rem(index, 2)),
        )

    def at_member(index):
        return (at_slide(z_hi, x, lax.rem(index, 2)), at_ctx(lax.div(index, 2), z_lo))

    work_peers = [works_on(lax.rem(work + by, slides)) for by in range(1, slides)]
    members = [at_member(lax.rem(member + by, ctxs)) for by in range(1, ctxs)]
    near = [
        (at_slide(z_hi, x, lax.rem(core + c, 2)), at_ctx(y + yy, lax.rem(z_lo + zz, 2)))
        for c in range(2) for yy in range(4) for zz in range(2) if (c, yy) != (0, 0)
    ]
    barrier = pltpu.get_barrier_semaphore()
    for peer in work_peers + near:
        pl.semaphore_signal(barrier, inc=1, device_id=peer, device_id_type=MESH)
    pl.semaphore_wait(barrier, len(work_peers) + len(near))

    def shard_of(relation, cc):
        zz = (1 - z_hi) if relation in (3, 4, 5, 7) else z_hi
        step = {0: 0, 1: -1, 2: 1, 3: 0, 4: -1, 5: 1, 6: 2, 7: 2}[relation]
        return at_slide(zz, x + step, cc)

    class Gather:
        def __init__(self, whole, depth, send, recv):
            self.whole, self.depth, self.send, self.recv = whole, depth, send, recv
            self.started = []

        def part(self, relation, cc, side=None):
            at = pl.ds(pl.multiple_of(shard_of(relation, cc) * self.depth, 16), self.depth)
            if side is None:
                return self.whole.at[at, :]
            cut = self.whole.shape[1] // 2
            return self.whole.at[at, pl.ds(side * cut, cut)]

        def handle(self, key, send_slot, slot, peer):
            part = self.part(*key)
            return pltpu.make_async_remote_copy(
                src_ref=part, dst_ref=part, send_sem=self.send.at[send_slot],
                recv_sem=self.recv.at[slot], device_id=peer, device_id_type=MESH,
            )

        def copy(self, key, peer, slot):
            self.handle(key, len(self.started), slot, peer).start()
            self.started.append(key)

        def arrive(self, key, slot):
            self.handle(key, 0, slot, sibling).wait_recv()

        def first(self):
            own = (0, core)
            self.copy(own, sibling, 8)
            self.copy(own, x_next, 1)
            self.copy(own, x_prev, 2)
            self.copy(own, zw_pair, 3)

        def second(self):
            for relation in (1, 2, 3):
                self.arrive((relation, core), relation)
            for relation in (1, 2, 3):
                self.copy((relation, core), sibling, 8 + relation)
            self.copy((1, core, 0), x_next, 6)
            self.copy((2, core, 1), x_prev, 0)
            self.copy((3, core), x_next, 4)
            self.copy((3, core), x_prev, 5)

        def third(self):
            self.arrive((6, core, 0), 6)
            self.arrive((6, core, 1), 0)
            self.copy((6, core), sibling, 14)
            self.copy((6, core), zw_pair, 7)

        def fourth(self):
            for relation in (4, 5, 7):
                self.arrive((relation, core), relation)
                self.copy((relation, core), sibling, 8 + relation)

        def last(self):
            for relation in range(8):
                self.arrive((relation, 1 - core), 8 + relation)

        def sent(self):
            for index, key in enumerate(self.started):
                self.handle(key, index, 0, sibling).wait_send()

    gather_a = Gather(w_a, wq.shape[0], a_send, a_recv)
    gather_b = Gather(w_b, wu.shape[0], b_send, b_recv)
    gather_c = Gather(w_c, wd.shape[0], c_send, c_recv)

    own48 = pl.ds(pl.multiple_of(slide * wq.shape[0], 16), wq.shape[0])
    w_a[own48, 0:width] = wq[...]
    w_a[own48, width:] = wkv[...]
    gather_a.first()
    lengths[0] = jnp.full(lengths.shape[1:], length_ref[0], jnp.int32)

    def length_handle():
        return pltpu.make_async_remote_copy(
            src_ref=lengths.at[0], dst_ref=lengths.at[1], send_sem=l_sem.at[0],
            recv_sem=l_sem.at[1], device_id=sibling, device_id_type=MESH,
        )

    length_handle().start()

    def grid(shape, dim):
        return lax.broadcasted_iota(jnp.int32, shape, dim)

    slots = tile_slot[...]
    devices = slides * ctxs
    share = block // devices
    owned = jnp.where((slots >> 9) == grid((devices, block), 0), 1.0, 0.0)
    earlier = jnp.where(grid((block, block), 0) < grid((block, block), 1), 1.0, 0.0).astype(bf16)
    ahead = dot(owned.astype(bf16), earlier)
    first_row = (grid((devices, block), 0) * share).astype(f32)
    target = jnp.sum(owned * (first_row + ahead), axis=0, keepdims=True)
    sorting = jnp.where(grid((block, block), 0).astype(f32) == target, 1.0, 0.0).astype(bf16)
    lane = grid((128, block), 0)
    digits = jnp.where(lane == 0, (slots >> 6) & 63, jnp.where(lane == 1, slots & 63, 0))
    outgoing[:, 0:width] = dot(sorting, tile_rows[...]).astype(bf16)
    outgoing[:, width:] = dot_nt(sorting, digits.astype(f32).astype(bf16)).astype(bf16)

    def pieces(buffer, index, depth):
        return buffer.at[pl.ds(pl.multiple_of(index * depth, 16), depth), :]

    slide_rows = block // slides

    def to_work(by):
        return pltpu.make_async_remote_copy(
            src_ref=pieces(outgoing, lax.rem(work + by, slides), slide_rows),
            dst_ref=pieces(in_slide, work, slide_rows), send_sem=s_send.at[by],
            recv_sem=s_recv.at[by], device_id=work_peers[by - 1], device_id_type=MESH,
        )

    def from_work(by):
        part = pieces(in_slide, lax.rem(work + slides - by, slides), slide_rows)
        return pltpu.make_async_remote_copy(
            src_ref=part, dst_ref=part, send_sem=s_send.at[by],
            recv_sem=s_recv.at[by], device_id=work_peers[by - 1], device_id_type=MESH,
        )

    for by in range(1, slides):
        to_work(by).start()
    own32 = pl.ds(pl.multiple_of(work * slide_rows, 16), slide_rows)
    in_slide[own32, :] = outgoing[own32, :]

    w_b[own48, 0:width] = wo[...]
    w_b[own48, width:] = wu[...]
    own192 = pl.ds(pl.multiple_of(slide * wd.shape[0], 16), wd.shape[0])
    w_c[own192, :] = wd[...]
    eye[...] = identity(width)
    q_aug[...] = jnp.zeros(q_aug.shape, bf16)
    q_aug[:, 128:144, :] = jnp.where(grid((pairs, 16, 2 * block), 1) == 0, 1.0, 0.0).astype(bf16)
    for v_buf in (v_even, v_odd):
        v_buf[:, 64:80, :] = jnp.where(grid((heads, 16, block), 1) == 0, 1.0, 0.0).astype(bf16)
    top[...] = jnp.full(top.shape, masked_score, f32)
    acc[...] = jnp.zeros(acc.shape, f32)
    gather_a.second()

    for by in range(1, slides):
        from_work(by).wait_recv()
    wanted = grid((block, block), 0)
    wanted = ((wanted >> 2) & 15) * slide_rows + (wanted >> 6) * share + (wanted & 3)
    turning = jnp.where(grid((block, block), 1) == wanted, 1.0, 0.0).astype(bf16)
    by_ctx[...] = dot(turning, in_slide[...]).astype(bf16)

    place = {key: index for index, key in enumerate(ORDER)}

    def chunk(relation, side):
        return rows.at[pl.ds(place[relation, side] * half, half), :]

    token_sends = []

    def rows_handle(source, target, send_slot, peer):
        return pltpu.make_async_remote_copy(
            src_ref=chunk(*source), dst_ref=chunk(*target), send_sem=t_send.at[send_slot],
            recv_sem=t_recv.at[place[target]], device_id=peer, device_id_type=MESH,
        )

    def pass_rows(source, relation, side, peer):
        rows_handle(source, (relation, side), len(token_sends), peer).start()
        token_sends.append(source)

    def rows_here(relation, side):
        rows_handle((relation, side), (relation, side), 0, sibling).wait_recv()

    for side in range(2):
        part = slice(side * half, (side + 1) * half)
        rows[part, :] = layer_norm(by_ctx[part, 0:width], gain1[...])
        pass_rows((0, side), 4, side, sibling)
        if side == 0:
            pass_rows((0, 0), 1, 0, y_next)
        else:
            pass_rows((0, 1), 2, 1, y_prev)
            pass_rows((0, 1), 1, 1, y_next)
            pass_rows((0, 0), 2, 0, y_prev)

    def positions(buffer):
        weight = grid((8, 128), 1)
        weight = jnp.where(weight == 0, 64.0, jnp.where(weight == 1, 1.0, 0.0)).astype(bf16)
        return dot_nt(weight, buffer[:, width:])

    length_handle().wait()
    valid = jnp.where(core == z_lo, lengths[0, 0:1, 0:1], lengths[1, 0:1, 0:1]).astype(f32)
    masked = jnp.where(positions(by_ctx) >= valid, masked_score, 0.0)
    masks[member, 0] = masked[:, 0:half]
    masks[member, 1] = masked[:, half:]

    def mask_handle(by, owner):
        return pltpu.make_async_remote_copy(
            src_ref=masks.at[owner], dst_ref=masks.at[owner], send_sem=m_send.at[by],
            recv_sem=m_recv.at[by], device_id=members[by - 1], device_id_type=MESH,
        )

    for by in range(1, ctxs):
        mask_handle(by, member).start()

    gather_a.third()
    gather_a.fourth()
    gather_b.first()
    gather_a.last()
    w_vt[...] = dot_nt(eye[...], w_a[:, 2 * width :]).astype(bf16)

    k_bufs, v_bufs, biases = (k_even, k_odd), (v_even, v_odd), (bias_even, bias_odd)

    def project(step, third, parity):
        here = rows[pl.ds(pl.multiple_of(step * block, block), block), :]
        span = pl.ds(pl.multiple_of(third * 256, 256), 256)
        key_span = pl.ds(pl.multiple_of(width + third * 256, 256), 256)
        k_bufs[parity][:, span] = dot(here, w_a[:, key_span]).astype(bf16)
        values_t = dot_nt(w_vt[span, :], here).astype(bf16)
        for at in range(4):
            v_bufs[parity][4 * third + at, 0:64, :] = values_t[at * 64 : at * 64 + 64, :]

    for third in range(3):
        project(0, third, 0)

    scale = HEAD_DIM ** (-0.5) * 1.4426950408889634
    queries = (dot(rows[0:block, :], w_a[:, 0:width]) * scale).astype(bf16)
    queries_t = dot_nt(eye[...], queries).astype(bf16)
    for head in range(heads):
        pair, at = head // 2, head % 2
        q_aug[pair, at * 64 : at * 64 + 64, at * block : (at + 1) * block] = queries_t[
            head * 64 : head * 64 + 64, :
        ]

    for by in range(1, ctxs):
        mask_handle(by, lax.rem(member + ctxs - by, ctxs)).wait_recv()

    def owner(relation):
        yy = lax.rem(y + {0: 0, 1: 3, 2: 1, 3: 2}[relation % 4], 4)
        return yy * 2 + ((1 - core) if relation >= 4 else core)

    def mask_column(first, first_side, second, second_side, parity):
        here = jnp.concatenate([masks[first, first_side], masks[second, second_side]], axis=1)
        here = jnp.concatenate([here, jnp.zeros((120, block), f32)], axis=0).astype(bf16)
        biases[parity][...] = dot_nt(eye[0:block, 0:block], here).astype(bf16)

    def score(pair, slot, parity):
        keys = k_bufs[parity][:, pl.ds(pl.multiple_of(pair * 128, 128), 128)]
        scores[slot] = dot(jnp.concatenate([keys, biases[parity][...]], axis=1), q_aug[pair])

    def soften(pair, slot, parity):
        before = top[pair]
        now = jnp.maximum(before, jnp.max(scores[slot], axis=0, keepdims=True))
        factor = jnp.exp2(before - now)
        top[pair] = now
        for side in range(2):
            span = slice(side * block, (side + 1) * block)
            weights = jnp.exp2(scores[slot, :, span] - now[:, span]).astype(bf16)
            head = 2 * pair + side
            acc[head] = acc[head] * factor[:, span] + dot(v_bufs[parity][head], weights)

    steps = len(ORDER) // 2
    firsts = [owner(ORDER[2 * step][0]) for step in range(steps)]
    seconds = [owner(ORDER[2 * step + 1][0]) for step in range(steps)]
    first_sides = [ORDER[2 * step][1] for step in range(steps)]
    second_sides = [ORDER[2 * step + 1][1] for step in range(steps)]

    def pick(options, step):
        chosen = options[0]
        for index in range(1, len(options)):
            chosen = jnp.where(step == index, options[index], chosen)
        return chosen

    def mask_of(step, parity):
        mask_column(
            pick(firsts, step), pick(first_sides, step), pick(seconds, step), pick(second_sides, step),
            parity,
        )

    def step_0():
        rows_here(4, 0)
        rows_here(4, 1)

    def step_1():
        rows_here(1, 0)
        pass_rows((1, 0), 5, 0, sibling)
        pass_rows((1, 0), 3, 0, y_next)
        rows_here(2, 1)
        pass_rows((2, 1), 6, 1, sibling)
        pass_rows((2, 1), 3, 1, y_prev)

    def step_2():
        rows_here(5, 0)
        rows_here(6, 1)
        gather_b.second()

    def step_3():
        rows_here(1, 1)
        pass_rows((1, 1), 5, 1, sibling)
        rows_here(2, 0)
        pass_rows((2, 0), 6, 0, sibling)
        gather_b.third()
        gather_c.first()

    def step_4():
        rows_here(5, 1)
        rows_here(6, 0)
        gather_b.fourth()

    def step_5():
        rows_here(3, 0)
        pass_rows((3, 0), 7, 0, sibling)
        rows_here(3, 1)
        pass_rows((3, 1), 7, 1, sibling)
        gather_c.second()

    def step_6():
        rows_here(7, 0)
        rows_here(7, 1)
        gather_c.third()

    def step_7():
        gather_c.fourth()

    events = [step_0, step_1, step_2, step_3, step_4, step_5, step_6, step_7]

    def turn(step, parity):
        for index in range(parity, steps, 2):
            pl.when(step == index)(events[index])
        later = jnp.minimum(step + 1, steps - 1)
        mask_of(later, 1 - parity)

        for third in range(3):
            project(later, third, 1 - parity)
            score(2 * third + 1, 1, parity)
            soften(2 * third, 0, parity)
            if third < 2:
                score(2 * third + 2, 0, parity)
            else:
                score(0, 0, 1 - parity)
            soften(2 * third + 1, 1, parity)

    def two_steps(index, _):
        turn(2 * index, 0)
        turn(2 * index + 1, 1)
        return 0

    mask_of(0, 0)
    score(0, 0, 0)
    lax.fori_loop(0, steps // 2, two_steps, 0)

    gather_b.last()
    for head in range(heads):
        done = acc[head]
        attended[head * 64 : head * 64 + 64, :] = (done[0:64] / done[64:65]).astype(bf16)
    turned = dot_nt(eye[0:block, 0:block], attended[...]).astype(bf16)
    mid = (by_ctx[:, 0:width].astype(f32) + dot(turned, w_b[:, 0:width])).astype(bf16)
    for index, source in enumerate(token_sends):
        rows_handle(source, source, index, sibling).wait_send()
    rows[0:block, :] = layer_norm(mid, gain2[...])
    down_acc[...] = mid.astype(f32)
    finished[:, width:] = by_ctx[:, width:]
    gather_c.last()

    tile = up_buf.shape[2]
    tiles = hidden // tile
    part_rows = block // 4
    ctx_rows = block // ctxs

    def send_home(target_ctx):
        return pltpu.make_async_remote_copy(
            src_ref=pieces(finished, target_ctx, ctx_rows), dst_ref=pieces(landed, member, ctx_rows),
            send_sem=f_send.at[target_ctx], recv_sem=f_recv.at[member],
            device_id=(at_slide(z_hi, x, z_lo), target_ctx), device_id_type=MESH,
        )

    def from_member(index):
        part = pieces(landed, index, ctx_rows)
        return pltpu.make_async_remote_copy(
            src_ref=part, dst_ref=part, send_sem=f_send.at[index], recv_sem=f_recv.at[index],
            device_id=sibling, device_id_type=MESH,
        )

    stays = core == z_lo

    def piece(index, _):
        yy = lax.rem(y + pick([2, 1, 3, 0], index), 4)
        here = pl.ds(pl.multiple_of(yy * part_rows, part_rows), part_rows)

        def up(at, slot):
            span = pl.ds(pl.multiple_of(width + at * tile, 128), tile)
            up_buf[slot] = dot(rows[here, :], w_b[:, span])

        def down(at, slot):
            active = jax.nn.gelu(up_buf[slot], approximate=True).astype(bf16)
            span = pl.ds(pl.multiple_of(at * tile, tile), tile)
            down_acc[here, :] += dot(active, w_c[span, :])

        up(0, 0)

        def two_tiles(at, _):
            up(2 * at + 1, 1)
            down(2 * at, 0)
            up(jnp.minimum(2 * at + 2, tiles - 1), 0)
            down(2 * at + 1, 1)
            return 0

        lax.fori_loop(0, tiles // 2, two_tiles, 0)
        finished[here, 0:width] = down_acc[here, :].astype(bf16)
        for zz in range(2):
            target = yy * 2 + zz
            home = stays & (yy == y) & (z_lo == zz)

            @pl.when(jnp.logical_not(home))
            def _():
                send_home(target).start()

            @pl.when(home)
            def _():
                at = pl.ds(pl.multiple_of(member * ctx_rows, 16), ctx_rows)
                landed[at, :] = finished[pl.ds(pl.multiple_of(target * ctx_rows, 16), ctx_rows), :]

        return 0

    lax.fori_loop(0, 4, piece, 0)

    for index in range(ctxs):
        @pl.when(jnp.logical_not(stays & (member == index)))
        def _():
            from_member(index).wait_recv()

    at_row = positions(landed)[0:1] - (ctx * block).astype(f32)
    placing = jnp.where(grid((block, block), 0).astype(f32) == at_row, 1.0, 0.0).astype(bf16)
    at = ctx * block + grid((block, width), 0)
    out[...] = jnp.where(at < length_ref[0], dot(placing, landed[:, 0:width]), 0.0).astype(bf16)

    for index in range(ctxs):
        @pl.when(jnp.logical_not(stays & (ctx == index)))
        def _():
            send_home(index).wait_send()

    for by in range(1, slides):
        to_work(by).wait_send()
    for by in range(1, ctxs):
        mask_handle(by, member).wait_send()
    for gather in (gather_a, gather_b, gather_c):
        gather.sent()


def on_device(
    tile_rows, tile_slot, lengths, ln_gain_attn, w_query, w_kv, w_out, ln_gain_mlp, w_up, w_down
):
    block, width = tile_rows.shape
    heads = width // HEAD_DIM
    hidden = w_up.shape[1]
    vmem = pl.BlockSpec(memory_space=pltpu.VMEM)
    dma = pltpu.SemaphoreType.DMA
    return pl.pallas_call(
        layer_kernel,
        out_shape=jax.ShapeDtypeStruct((block, width), bf16),
        in_specs=[vmem, vmem, pl.BlockSpec(memory_space=pltpu.SMEM)] + [vmem] * 7,
        out_specs=vmem,
        scratch_shapes=[
            pltpu.VMEM((block, width + 128), bf16),
            pltpu.VMEM((block, width + 128), bf16),
            pltpu.VMEM((block, width + 128), bf16),
            pltpu.VMEM((block, width + 128), bf16),
            pltpu.VMEM((block, width + 128), bf16),
            pltpu.VMEM((2, 8, 128), jnp.int32),
            pltpu.VMEM((8, 2, 8, block // 2), f32),
            pltpu.VMEM((width, width), bf16),
            pltpu.VMEM((8 * block, width), bf16),
            pltpu.VMEM((width, 3 * width), bf16),
            pltpu.VMEM((width, width + hidden), bf16),
            pltpu.VMEM((hidden, width), bf16),
            pltpu.VMEM((width, width), bf16),
            pltpu.VMEM((heads // 2, 256, 2 * block), bf16),
            pltpu.VMEM((block, width), bf16),
            pltpu.VMEM((block, width), bf16),
            pltpu.VMEM((heads, value_rows, block), bf16),
            pltpu.VMEM((heads, value_rows, block), bf16),
            pltpu.VMEM((block, 128), bf16),
            pltpu.VMEM((block, 128), bf16),
            pltpu.VMEM((2, block, 2 * block), f32),
            pltpu.VMEM((heads // 2, 1, 2 * block), f32),
            pltpu.VMEM((heads, value_rows, block), f32),
            pltpu.VMEM((width, block), bf16),
            pltpu.VMEM((2, block // 4, 512), f32),
            pltpu.VMEM((block, width), f32),
            dma((16,)), dma((16,)),
            dma((8,)), dma((8,)),
            dma((8,)), dma((8,)),
            dma((2,)),
            dma((14,)), dma((16,)),
            dma((16,)), dma((16,)),
            dma((16,)), dma((16,)),
            dma((16,)), dma((16,)),
        ],
        compiler_params=pltpu.CompilerParams(
            collective_id=0, has_side_effects=True, vmem_limit_bytes=60 * 2**20
        ),
        name="layer",
    )(
        tile_rows, tile_slot, lengths, ln_gain_attn, w_query, w_kv, w_out,
        ln_gain_mlp, w_up, w_down,
    )


def solution(mesh):
    return jax.shard_map(
        on_device,
        mesh=mesh,
        in_specs=(
            P(("slide", "ctx"), None),
            P(("slide", "ctx"), None),
            P("slide"),
            P(),
            P("slide", None),
            P("slide", None),
            P("slide", None),
            P(),
            P("slide", None),
            P("slide", None),
        ),
        out_specs=P(("slide", "ctx"), None),
        check_vma=False,
    )
```

```python
import functools

import jax
import jax.numpy as jnp
from jax import lax
from jax.experimental import pallas as pl
from jax.experimental.pallas import tpu as pltpu
from jax.sharding import PartitionSpec as P

HEAD_DIM = 64
MESH = pl.DeviceIdType.MESH
bf16, f32 = jnp.bfloat16, jnp.float32

norm_eps = 1e-05
masked_score = -1e30
value_rows = 80
ORDER = [
    (0, 0), (0, 1), (4, 0), (4, 1), (1, 0), (2, 1), (5, 0), (6, 1),
    (1, 1), (2, 0), (5, 1), (6, 0), (3, 0), (3, 1), (7, 0), (7, 1),
]


def layer_norm(rows, gain):
    values32 = rows.astype(f32)
    row_mean = jnp.mean(values32, axis=-1, keepdims=True)
    centred = values32 - row_mean
    row_var = jnp.mean(centred * centred, axis=-1, keepdims=True)
    return (centred * lax.rsqrt(row_var + norm_eps) * gain).astype(bf16)


def dot(left, right):
    return jnp.dot(left, right, preferred_element_type=f32)


def dot_nt(left, right):
    return lax.dot_general(left, right, (((1,), (1,)), ((), ())), preferred_element_type=f32)


def identity(size):
    row = lax.broadcasted_iota(jnp.int32, (size, size), 0)
    column = lax.broadcasted_iota(jnp.int32, (size, size), 1)
    return jnp.where(row == column, 1.0, 0.0).astype(bf16)


def layer_kernel(
    tile_rows, tile_slot, length_ref, gain1, wq, wkv, wo, gain2, wu, wd,
    out,
    outgoing, in_slide, by_ctx, finished, landed, lengths, masks, eye,
    rows, w_a, w_b, w_c, w_vt, q_aug, k_even, k_odd, v_even, v_odd, bias_even, bias_odd, scores, top, acc, attended, up_buf, down_acc,
    s_send, s_recv, f_send, f_recv, m_send, m_recv, l_sem, t_send, t_recv, a_send, a_recv, b_send, b_recv, c_send, c_recv,
):
    block, width = tile_rows.shape
    half = block // 2
    heads = width // HEAD_DIM
    pairs = heads // 2
    hidden = wu.shape[1]
    slide = lax.axis_index("slide")
    ctx = lax.axis_index("ctx")
    z_hi, x, core = lax.div(slide, 8), lax.rem(lax.div(slide, 2), 4), lax.rem(slide, 2)
    y, z_lo = lax.div(ctx, 2), lax.rem(ctx, 2)

    def at_slide(zz, xx, cc):
        return zz * 8 + lax.rem(xx + 4, 4) * 2 + cc

    def at_ctx(yy, zz):
        return lax.rem(yy + 4, 4) * 2 + zz

    slides, ctxs = 16, 8
    y_next = (slide, at_ctx(y + 1, z_lo))
    y_prev = (slide, at_ctx(y - 1, z_lo))
    x_next = (at_slide(z_hi, x + 1, core), ctx)
    x_prev = (at_slide(z_hi, x - 1, core), ctx)
    zw_pair = (at_slide(1 - z_hi, x, core), at_ctx(y, 1 - z_lo))
    sibling = (at_slide(z_hi, x, 1 - core), ctx)

    work = at_slide(z_hi, x, z_lo)
    member = y * 2 + core

    def works_on(index):
        return (
            at_slide(lax.div(index, 8), lax.rem(lax.div(index, 2), 4), core),
            at_ctx(y, lax.rem(index, 2)),
        )

    def at_member(index):
        return (at_slide(z_hi, x, lax.rem(index, 2)), at_ctx(lax.div(index, 2), z_lo))

    work_peers = [works_on(lax.rem(work + by, slides)) for by in range(1, slides)]
    members = [at_member(lax.rem(member + by, ctxs)) for by in range(1, ctxs)]
    near = [
        (at_slide(z_hi, x, lax.rem(core + c, 2)), at_ctx(y + yy, lax.rem(z_lo + zz, 2)))
        for c in range(2) for yy in range(4) for zz in range(2) if (c, yy) != (0, 0)
    ]
    barrier = pltpu.get_barrier_semaphore()
    for peer in work_peers + near:
        pl.semaphore_signal(barrier, inc=1, device_id=peer, device_id_type=MESH)
    pl.semaphore_wait(barrier, len(work_peers) + len(near))

    def shard_of(relation, cc):
        zz = (1 - z_hi) if relation in (3, 4, 5, 7) else z_hi
        step = {0: 0, 1: -1, 2: 1, 3: 0, 4: -1, 5: 1, 6: 2, 7: 2}[relation]
        return at_slide(zz, x + step, cc)

    x_far = (at_slide(z_hi, x + 2, core), ctx)

    class Gather:
        def __init__(self, whole, depth, send, recv, direct, split):
            self.whole, self.depth, self.send, self.recv = whole, depth, send, recv
            self.direct, self.split = direct, split
            self.started = []

        def part(self, relation, cc, columns):
            at = pl.ds(pl.multiple_of(shard_of(relation, cc) * self.depth, 16), self.depth)
            cut = self.whole.shape[1] // 2
            if columns == "all" or (columns == "mine" and not self.split):
                return self.whole.at[at, :]
            if columns in (0, 1):
                return self.whole.at[at, pl.ds(columns * cut, cut)]
            side = lax.rem(y, 2) if columns == "mine" else 1 - lax.rem(y, 2)
            return self.whole.at[at, pl.ds(pl.multiple_of(side * cut, 128), cut)]

        def handle(self, key, send_slot, slot, peer):
            part = self.part(*key)
            return pltpu.make_async_remote_copy(
                src_ref=part, dst_ref=part, send_sem=self.send.at[send_slot],
                recv_sem=self.recv.at[slot], device_id=peer, device_id_type=MESH,
            )

        def copy(self, key, peer, slot):
            self.handle(key, len(self.started), slot, peer).start()
            self.started.append(key)

        def arrive(self, key, slot):
            self.handle(key, 0, slot, sibling).wait_recv()

        def share(self, relation):
            key = (relation, core, "mine")
            self.copy(key, sibling, 8 + relation)
            if self.split:
                self.copy(key, y_next if relation % 2 else y_prev, 16 + relation)

        def first(self):
            self.copy((0, core, "all"), sibling, 8)
            own = (0, core, "mine")
            self.copy(own, x_next, 1)
            self.copy(own, x_prev, 2)
            self.copy(own, zw_pair, 3)
            if self.direct:
                self.copy(own, x_far, 6)

        def second(self):
            for relation in (1, 2, 3):
                self.arrive((relation, core, "mine"), relation)
                self.share(relation)
            if not self.direct:
                self.copy((1, core, 0), x_next, 6)
                self.copy((2, core, 1), x_prev, 0)
            self.copy((3, core, "mine"), x_next, 4)
            self.copy((3, core, "mine"), x_prev, 5)
            if self.direct:
                self.third()

        def third(self):
            if self.direct:
                self.arrive((6, core, "mine"), 6)
            else:
                self.arrive((6, core, 0), 6)
                self.arrive((6, core, 1), 0)
            self.share(6)
            self.copy((6, core, "mine"), zw_pair, 7)

        def fourth(self):
            for relation in (4, 5, 7):
                self.arrive((relation, core, "mine"), relation)
                self.share(relation)

        def fifth(self):
            for relation in range(1, 8):
                self.arrive((relation, core, "other"), 16 + relation)
                self.copy((relation, core, "other"), sibling, 24 + relation)

        def last(self):
            self.arrive((0, 1 - core, "all"), 8)
            for relation in range(1, 8):
                self.arrive((relation, 1 - core, "mine"), 8 + relation)
                if self.split:
                    self.arrive((relation, 1 - core, "other"), 24 + relation)

        def sent(self):
            for index, key in enumerate(self.started):
                self.handle(key, index, 0, sibling).wait_send()

    gather_a = Gather(w_a, wq.shape[0], a_send, a_recv, True, True)
    gather_b = Gather(w_b, wu.shape[0], b_send, b_recv, False, False)
    gather_c = Gather(w_c, wd.shape[0], c_send, c_recv, True, False)

    own48 = pl.ds(pl.multiple_of(slide * wq.shape[0], 16), wq.shape[0])
    w_a[own48, 0:width] = wq[...]
    w_a[own48, width:] = wkv[...]
    gather_a.first()
    lengths[0] = jnp.full(lengths.shape[1:], length_ref[0], jnp.int32)

    def length_handle():
        return pltpu.make_async_remote_copy(
            src_ref=lengths.at[0], dst_ref=lengths.at[1], send_sem=l_sem.at[0],
            recv_sem=l_sem.at[1], device_id=sibling, device_id_type=MESH,
        )

    length_handle().start()

    def grid(shape, dim):
        return lax.broadcasted_iota(jnp.int32, shape, dim)

    slots = tile_slot[...]
    devices = slides * ctxs
    share = block // devices
    owned = jnp.where((slots >> 9) == grid((devices, block), 0), 1.0, 0.0)
    earlier = jnp.where(grid((block, block), 0) < grid((block, block), 1), 1.0, 0.0).astype(bf16)
    ahead = dot(owned.astype(bf16), earlier)
    first_row = (grid((devices, block), 0) * share).astype(f32)
    target = jnp.sum(owned * (first_row + ahead), axis=0, keepdims=True)
    sorting = jnp.where(grid((block, block), 0).astype(f32) == target, 1.0, 0.0).astype(bf16)
    lane = grid((128, block), 0)
    digits = jnp.where(lane == 0, (slots >> 6) & 63, jnp.where(lane == 1, slots & 63, 0))
    outgoing[:, 0:width] = dot(sorting, tile_rows[...]).astype(bf16)
    outgoing[:, width:] = dot_nt(sorting, digits.astype(f32).astype(bf16)).astype(bf16)

    def pieces(buffer, index, depth):
        return buffer.at[pl.ds(pl.multiple_of(index * depth, 16), depth), :]

    slide_rows = block // slides

    def to_work(by):
        return pltpu.make_async_remote_copy(
            src_ref=pieces(outgoing, lax.rem(work + by, slides), slide_rows),
            dst_ref=pieces(in_slide, work, slide_rows), send_sem=s_send.at[by],
            recv_sem=s_recv.at[by], device_id=work_peers[by - 1], device_id_type=MESH,
        )

    def from_work(by):
        part = pieces(in_slide, lax.rem(work + slides - by, slides), slide_rows)
        return pltpu.make_async_remote_copy(
            src_ref=part, dst_ref=part, send_sem=s_send.at[by],
            recv_sem=s_recv.at[by], device_id=work_peers[by - 1], device_id_type=MESH,
        )

    for by in range(1, slides):
        to_work(by).start()
    own32 = pl.ds(pl.multiple_of(work * slide_rows, 16), slide_rows)
    in_slide[own32, :] = outgoing[own32, :]

    w_b[own48, 0:width] = wo[...]
    w_b[own48, width:] = wu[...]
    own192 = pl.ds(pl.multiple_of(slide * wd.shape[0], 16), wd.shape[0])
    w_c[own192, :] = wd[...]
    eye[...] = identity(width)
    q_aug[...] = jnp.zeros(q_aug.shape, bf16)
    q_aug[:, 128:144, :] = jnp.where(grid((pairs, 16, 2 * block), 1) == 0, 1.0, 0.0).astype(bf16)
    for v_buf in (v_even, v_odd):
        v_buf[:, 64:80, :] = jnp.where(grid((heads, 16, block), 1) == 0, 1.0, 0.0).astype(bf16)
    top[...] = jnp.full(top.shape, masked_score, f32)
    acc[...] = jnp.zeros(acc.shape, f32)
    gather_a.second()

    for by in range(1, slides):
        from_work(by).wait_recv()
    wanted = grid((block, block), 0)
    wanted = ((wanted >> 2) & 15) * slide_rows + (wanted >> 6) * share + (wanted & 3)
    turning = jnp.where(grid((block, block), 1) == wanted, 1.0, 0.0).astype(bf16)
    by_ctx[...] = dot(turning, in_slide[...]).astype(bf16)

    place = {key: index for index, key in enumerate(ORDER)}

    def chunk(relation, side):
        return rows.at[pl.ds(place[relation, side] * half, half), :]

    token_sends = []

    def rows_handle(source, target, send_slot, peer):
        return pltpu.make_async_remote_copy(
            src_ref=chunk(*source), dst_ref=chunk(*target), send_sem=t_send.at[send_slot],
            recv_sem=t_recv.at[place[target]], device_id=peer, device_id_type=MESH,
        )

    def pass_rows(source, relation, side, peer):
        rows_handle(source, (relation, side), len(token_sends), peer).start()
        token_sends.append(source)

    def rows_here(relation, side):
        rows_handle((relation, side), (relation, side), 0, sibling).wait_recv()

    for side in range(2):
        part = slice(side * half, (side + 1) * half)
        rows[part, :] = layer_norm(by_ctx[part, 0:width], gain1[...])
        pass_rows((0, side), 4, side, sibling)
        if side == 0:
            pass_rows((0, 0), 1, 0, y_next)
        else:
            pass_rows((0, 1), 2, 1, y_prev)

    def positions(buffer):
        weight = grid((8, 128), 1)
        weight = jnp.where(weight == 0, 64.0, jnp.where(weight == 1, 1.0, 0.0)).astype(bf16)
        return dot_nt(weight, buffer[:, width:])

    length_handle().wait()
    valid = jnp.where(core == z_lo, lengths[0, 0:1, 0:1], lengths[1, 0:1, 0:1]).astype(f32)
    masked = jnp.where(positions(by_ctx) >= valid, masked_score, 0.0)
    masks[member, 0] = masked[:, 0:half]
    masks[member, 1] = masked[:, half:]

    def mask_handle(by, owner):
        return pltpu.make_async_remote_copy(
            src_ref=masks.at[owner], dst_ref=masks.at[owner], send_sem=m_send.at[by],
            recv_sem=m_recv.at[by], device_id=members[by - 1], device_id_type=MESH,
        )

    for by in range(1, ctxs):
        mask_handle(by, member).start()

    gather_a.fourth()
    gather_b.first()
    gather_a.fifth()
    gather_a.last()
    w_vt[...] = dot_nt(eye[...], w_a[:, 2 * width :]).astype(bf16)

    k_bufs, v_bufs, biases = (k_even, k_odd), (v_even, v_odd), (bias_even, bias_odd)

    def project(step, third, parity):
        here = rows[pl.ds(pl.multiple_of(step * block, block), block), :]
        span = pl.ds(pl.multiple_of(third * 256, 256), 256)
        key_span = pl.ds(pl.multiple_of(width + third * 256, 256), 256)
        k_bufs[parity][:, span] = dot(here, w_a[:, key_span]).astype(bf16)
        values_t = dot_nt(w_vt[span, :], here).astype(bf16)
        for at in range(4):
            v_bufs[parity][4 * third + at, 0:64, :] = values_t[at * 64 : at * 64 + 64, :]

    for third in range(3):
        project(0, third, 0)

    scale = HEAD_DIM ** (-0.5) * 1.4426950408889634
    queries = (dot(rows[0:block, :], w_a[:, 0:width]) * scale).astype(bf16)
    queries_t = dot_nt(eye[...], queries).astype(bf16)
    for head in range(heads):
        pair, at = head // 2, head % 2
        q_aug[pair, at * 64 : at * 64 + 64, at * block : (at + 1) * block] = queries_t[
            head * 64 : head * 64 + 64, :
        ]

    for by in range(1, ctxs):
        mask_handle(by, lax.rem(member + ctxs - by, ctxs)).wait_recv()

    def owner(relation):
        yy = lax.rem(y + {0: 0, 1: 3, 2: 1, 3: 2}[relation % 4], 4)
        return yy * 2 + ((1 - core) if relation >= 4 else core)

    def mask_column(first, first_side, second, second_side, parity):
        here = jnp.concatenate([masks[first, first_side], masks[second, second_side]], axis=1)
        here = jnp.concatenate([here, jnp.zeros((120, block), f32)], axis=0).astype(bf16)
        biases[parity][...] = dot_nt(eye[0:block, 0:block], here).astype(bf16)

    def score(pair, slot, parity):
        keys = k_bufs[parity][:, pl.ds(pl.multiple_of(pair * 128, 128), 128)]
        scores[slot] = dot(jnp.concatenate([keys, biases[parity][...]], axis=1), q_aug[pair])

    def soften(pair, slot, parity):
        before = top[pair]
        now = jnp.maximum(before, jnp.max(scores[slot], axis=0, keepdims=True))
        factor = jnp.exp2(before - now)
        top[pair] = now
        for side in range(2):
            span = slice(side * block, (side + 1) * block)
            weights = jnp.exp2(scores[slot, :, span] - now[:, span]).astype(bf16)
            head = 2 * pair + side
            acc[head] = acc[head] * factor[:, span] + dot(v_bufs[parity][head], weights)

    steps = len(ORDER) // 2
    firsts = [owner(ORDER[2 * step][0]) for step in range(steps)]
    seconds = [owner(ORDER[2 * step + 1][0]) for step in range(steps)]
    first_sides = [ORDER[2 * step][1] for step in range(steps)]
    second_sides = [ORDER[2 * step + 1][1] for step in range(steps)]

    def pick(options, step):
        chosen = options[0]
        for index in range(1, len(options)):
            chosen = jnp.where(step == index, options[index], chosen)
        return chosen

    def mask_of(step, parity):
        mask_column(
            pick(firsts, step), pick(first_sides, step), pick(seconds, step), pick(second_sides, step),
            parity,
        )

    def step_0():
        rows_here(4, 0)
        rows_here(4, 1)
        pass_rows((0, 1), 1, 1, y_next)
        pass_rows((0, 0), 2, 0, y_prev)
        gather_c.first()

    def step_1():
        rows_here(1, 0)
        pass_rows((1, 0), 5, 0, sibling)
        pass_rows((1, 0), 3, 0, y_next)
        rows_here(2, 1)
        pass_rows((2, 1), 6, 1, sibling)
        pass_rows((2, 1), 3, 1, y_prev)

    def step_2():
        rows_here(5, 0)
        rows_here(6, 1)
        gather_b.second()

    def step_3():
        rows_here(1, 1)
        pass_rows((1, 1), 5, 1, sibling)
        rows_here(2, 0)
        pass_rows((2, 0), 6, 0, sibling)

    def step_4():
        rows_here(5, 1)
        rows_here(6, 0)
        gather_c.second()

    def step_5():
        rows_here(3, 0)
        pass_rows((3, 0), 7, 0, sibling)
        rows_here(3, 1)
        pass_rows((3, 1), 7, 1, sibling)

    def step_6():
        rows_here(7, 0)
        rows_here(7, 1)
        gather_b.third()

    def step_7():
        pass

    events = [step_0, step_1, step_2, step_3, step_4, step_5, step_6, step_7]

    def turn(step, parity):
        for index in range(parity, steps, 2):
            pl.when(step == index)(events[index])
        later = jnp.minimum(step + 1, steps - 1)
        mask_of(later, 1 - parity)

        for third in range(3):
            project(later, third, 1 - parity)
            score(2 * third + 1, 1, parity)
            soften(2 * third, 0, parity)
            if third < 2:
                score(2 * third + 2, 0, parity)
            else:
                score(0, 0, 1 - parity)
            soften(2 * third + 1, 1, parity)

    def two_steps(index, _):
        turn(2 * index, 0)
        turn(2 * index + 1, 1)
        return 0

    mask_of(0, 0)
    score(0, 0, 0)
    lax.fori_loop(0, steps // 2, two_steps, 0)

    gather_b.fourth()
    gather_c.fourth()
    for head in range(heads):
        done = acc[head]
        attended[head * 64 : head * 64 + 64, :] = (done[0:64] / done[64:65]).astype(bf16)
    gather_b.last()
    turned = dot_nt(eye[0:block, 0:block], attended[...]).astype(bf16)
    mid = (by_ctx[:, 0:width].astype(f32) + dot(turned, w_b[:, 0:width])).astype(bf16)
    for index, source in enumerate(token_sends):
        rows_handle(source, source, index, sibling).wait_send()
    rows[0:block, :] = layer_norm(mid, gain2[...])
    down_acc[...] = mid.astype(f32)
    finished[:, width:] = by_ctx[:, width:]
    gather_c.last()

    tile = up_buf.shape[2]
    tiles = hidden // tile
    part_rows = block // 4
    ctx_rows = block // ctxs

    def send_home(target_ctx):
        return pltpu.make_async_remote_copy(
            src_ref=pieces(finished, target_ctx, ctx_rows), dst_ref=pieces(landed, member, ctx_rows),
            send_sem=f_send.at[target_ctx], recv_sem=f_recv.at[member],
            device_id=(at_slide(z_hi, x, z_lo), target_ctx), device_id_type=MESH,
        )

    def from_member(index):
        part = pieces(landed, index, ctx_rows)
        return pltpu.make_async_remote_copy(
            src_ref=part, dst_ref=part, send_sem=f_send.at[index], recv_sem=f_recv.at[index],
            device_id=sibling, device_id_type=MESH,
        )

    stays = core == z_lo

    def piece(index, _):
        yy = lax.rem(y + pick([2, 1, 3, 0], index), 4)
        here = pl.ds(pl.multiple_of(yy * part_rows, part_rows), part_rows)

        def up(at, slot):
            span = pl.ds(pl.multiple_of(width + at * tile, 128), tile)
            up_buf[slot] = dot(rows[here, :], w_b[:, span])

        def down(at, slot):
            active = jax.nn.gelu(up_buf[slot], approximate=True).astype(bf16)
            span = pl.ds(pl.multiple_of(at * tile, tile), tile)
            down_acc[here, :] += dot(active, w_c[span, :])

        up(0, 0)

        def two_tiles(at, _):
            up(2 * at + 1, 1)
            down(2 * at, 0)
            up(jnp.minimum(2 * at + 2, tiles - 1), 0)
            down(2 * at + 1, 1)
            return 0

        lax.fori_loop(0, tiles // 2, two_tiles, 0)
        finished[here, 0:width] = down_acc[here, :].astype(bf16)
        for zz in range(2):
            target = yy * 2 + zz
            home = stays & (yy == y) & (z_lo == zz)

            @pl.when(jnp.logical_not(home))
            def _():
                send_home(target).start()

            @pl.when(home)
            def _():
                at = pl.ds(pl.multiple_of(member * ctx_rows, 16), ctx_rows)
                landed[at, :] = finished[pl.ds(pl.multiple_of(target * ctx_rows, 16), ctx_rows), :]

        return 0

    lax.fori_loop(0, 4, piece, 0)

    for index in range(ctxs):
        @pl.when(jnp.logical_not(stays & (member == index)))
        def _():
            from_member(index).wait_recv()

    at_row = positions(landed)[0:1] - (ctx * block).astype(f32)
    placing = jnp.where(grid((block, block), 0).astype(f32) == at_row, 1.0, 0.0).astype(bf16)
    at = ctx * block + grid((block, width), 0)
    out[...] = jnp.where(at < length_ref[0], dot(placing, landed[:, 0:width]), 0.0).astype(bf16)

    for index in range(ctxs):
        @pl.when(jnp.logical_not(stays & (ctx == index)))
        def _():
            send_home(index).wait_send()

    for by in range(1, slides):
        to_work(by).wait_send()
    for by in range(1, ctxs):
        mask_handle(by, member).wait_send()
    for gather in (gather_a, gather_b, gather_c):
        gather.sent()


def on_device(
    tile_rows, tile_slot, lengths, ln_gain_attn, w_query, w_kv, w_out, ln_gain_mlp, w_up, w_down
):
    block, width = tile_rows.shape
    heads = width // HEAD_DIM
    hidden = w_up.shape[1]
    vmem = pl.BlockSpec(memory_space=pltpu.VMEM)
    dma = pltpu.SemaphoreType.DMA
    return pl.pallas_call(
        layer_kernel,
        out_shape=jax.ShapeDtypeStruct((block, width), bf16),
        in_specs=[vmem, vmem, pl.BlockSpec(memory_space=pltpu.SMEM)] + [vmem] * 7,
        out_specs=vmem,
        scratch_shapes=[
            pltpu.VMEM((block, width + 128), bf16),
            pltpu.VMEM((block, width + 128), bf16),
            pltpu.VMEM((block, width + 128), bf16),
            pltpu.VMEM((block, width + 128), bf16),
            pltpu.VMEM((block, width + 128), bf16),
            pltpu.VMEM((2, 8, 128), jnp.int32),
            pltpu.VMEM((8, 2, 8, block // 2), f32),
            pltpu.VMEM((width, width), bf16),
            pltpu.VMEM((8 * block, width), bf16),
            pltpu.VMEM((width, 3 * width), bf16),
            pltpu.VMEM((width, width + hidden), bf16),
            pltpu.VMEM((hidden, width), bf16),
            pltpu.VMEM((width, width), bf16),
            pltpu.VMEM((heads // 2, 256, 2 * block), bf16),
            pltpu.VMEM((block, width), bf16),
            pltpu.VMEM((block, width), bf16),
            pltpu.VMEM((heads, value_rows, block), bf16),
            pltpu.VMEM((heads, value_rows, block), bf16),
            pltpu.VMEM((block, 128), bf16),
            pltpu.VMEM((block, 128), bf16),
            pltpu.VMEM((2, block, 2 * block), f32),
            pltpu.VMEM((heads // 2, 1, 2 * block), f32),
            pltpu.VMEM((heads, value_rows, block), f32),
            pltpu.VMEM((width, block), bf16),
            pltpu.VMEM((2, block // 4, 512), f32),
            pltpu.VMEM((block, width), f32),
            dma((16,)), dma((16,)),
            dma((8,)), dma((8,)),
            dma((8,)), dma((8,)),
            dma((2,)),
            dma((14,)), dma((16,)),
            dma((32,)), dma((32,)),
            dma((16,)), dma((16,)),
            dma((16,)), dma((16,)),
        ],
        compiler_params=pltpu.CompilerParams(
            collective_id=0, has_side_effects=True, vmem_limit_bytes=60 * 2**20
        ),
        name="layer",
    )(
        tile_rows, tile_slot, lengths, ln_gain_attn, w_query, w_kv, w_out,
        ln_gain_mlp, w_up, w_down,
    )


def solution(mesh):
    return jax.shard_map(
        on_device,
        mesh=mesh,
        in_specs=(
            P(("slide", "ctx"), None),
            P(("slide", "ctx"), None),
            P("slide"),
            P(),
            P("slide", None),
            P("slide", None),
            P("slide", None),
            P(),
            P("slide", None),
            P("slide", None),
        ),
        out_specs=P(("slide", "ctx"), None),
        check_vma=False,
    )
```

```python
import functools

import jax
import jax.numpy as jnp
from jax import lax
from jax.experimental import pallas as pl
from jax.experimental.pallas import tpu as pltpu
from jax.sharding import PartitionSpec as P

HEAD_DIM = 64
MESH = pl.DeviceIdType.MESH
bf16, f32 = jnp.bfloat16, jnp.float32

norm_eps = 1e-05
masked_score = -1e30
value_rows = 80
ORDER = [
    (0, 0), (0, 1), (4, 0), (4, 1), (1, 0), (2, 1), (5, 0), (6, 1),
    (1, 1), (2, 0), (5, 1), (6, 0), (3, 0), (3, 1), (7, 0), (7, 1),
]


def layer_norm(rows, gain):
    values32 = rows.astype(f32)
    row_mean = jnp.mean(values32, axis=-1, keepdims=True)
    centred = values32 - row_mean
    row_var = jnp.mean(centred * centred, axis=-1, keepdims=True)
    return (centred * lax.rsqrt(row_var + norm_eps) * gain).astype(bf16)


def dot(left, right):
    return jnp.dot(left, right, preferred_element_type=f32)


def dot_nt(left, right):
    return lax.dot_general(left, right, (((1,), (1,)), ((), ())), preferred_element_type=f32)


def identity(size):
    row = lax.broadcasted_iota(jnp.int32, (size, size), 0)
    column = lax.broadcasted_iota(jnp.int32, (size, size), 1)
    return jnp.where(row == column, 1.0, 0.0).astype(bf16)


def layer_kernel(
    tile_rows, tile_slot, length_ref, gain1, wq, wkv, wo, gain2, wu, wd,
    out,
    outgoing, in_slide, by_ctx, finished, landed, lengths, masks, eye,
    rows, w_a, w_b, w_c, w_vt, q_aug, k_even, k_odd, v_even, v_odd, bias_even, bias_odd, scores, top, acc, attended, up_buf, down_acc,
    s_send, s_recv, f_send, f_recv, m_send, m_recv, l_sem, t_send, t_recv, a_send, a_recv, b_send, b_recv, c_send, c_recv,
):
    block, width = tile_rows.shape
    half = block // 2
    heads = width // HEAD_DIM
    pairs = heads // 2
    hidden = wu.shape[1]
    slide = lax.axis_index("slide")
    ctx = lax.axis_index("ctx")
    z_hi, x, core = lax.div(slide, 8), lax.rem(lax.div(slide, 2), 4), lax.rem(slide, 2)
    y, z_lo = lax.div(ctx, 2), lax.rem(ctx, 2)

    def at_slide(zz, xx, cc):
        return zz * 8 + lax.rem(xx + 4, 4) * 2 + cc

    def at_ctx(yy, zz):
        return lax.rem(yy + 4, 4) * 2 + zz

    slides, ctxs = 16, 8
    y_next = (slide, at_ctx(y + 1, z_lo))
    y_prev = (slide, at_ctx(y - 1, z_lo))
    x_next = (at_slide(z_hi, x + 1, core), ctx)
    x_prev = (at_slide(z_hi, x - 1, core), ctx)
    zw_pair = (at_slide(1 - z_hi, x, core), at_ctx(y, 1 - z_lo))
    sibling = (at_slide(z_hi, x, 1 - core), ctx)

    work = at_slide(z_hi, x, z_lo)
    member = y * 2 + core

    def works_on(index):
        return (
            at_slide(lax.div(index, 8), lax.rem(lax.div(index, 2), 4), core),
            at_ctx(y, lax.rem(index, 2)),
        )

    def at_member(index):
        return (at_slide(z_hi, x, lax.rem(index, 2)), at_ctx(lax.div(index, 2), z_lo))

    work_peers = [works_on(lax.rem(work + by, slides)) for by in range(1, slides)]
    members = [at_member(lax.rem(member + by, ctxs)) for by in range(1, ctxs)]
    near = [
        (at_slide(z_hi, x, lax.rem(core + c, 2)), at_ctx(y + yy, lax.rem(z_lo + zz, 2)))
        for c in range(2) for yy in range(4) for zz in range(2) if (c, yy) != (0, 0)
    ]
    barrier = pltpu.get_barrier_semaphore()
    for peer in work_peers + near:
        pl.semaphore_signal(barrier, inc=1, device_id=peer, device_id_type=MESH)

    def shard_of(relation, cc):
        zz = (1 - z_hi) if relation in (3, 4, 5, 7) else z_hi
        step = {0: 0, 1: -1, 2: 1, 3: 0, 4: -1, 5: 1, 6: 2, 7: 2}[relation]
        return at_slide(zz, x + step, cc)

    x_far = (at_slide(z_hi, x + 2, core), ctx)

    class Gather:
        def __init__(self, whole, depth, send, recv, direct, split):
            self.whole, self.depth, self.send, self.recv = whole, depth, send, recv
            self.direct, self.split = direct, split
            self.started = []

        def part(self, relation, cc, columns):
            at = pl.ds(pl.multiple_of(shard_of(relation, cc) * self.depth, 16), self.depth)
            cut = self.whole.shape[1] // 2
            if columns == "all" or (columns == "mine" and not self.split):
                return self.whole.at[at, :]
            if columns in (0, 1):
                return self.whole.at[at, pl.ds(columns * cut, cut)]
            side = lax.rem(y, 2) if columns == "mine" else 1 - lax.rem(y, 2)
            return self.whole.at[at, pl.ds(pl.multiple_of(side * cut, 128), cut)]

        def handle(self, key, send_slot, slot, peer):
            part = self.part(*key)
            return pltpu.make_async_remote_copy(
                src_ref=part, dst_ref=part, send_sem=self.send.at[send_slot],
                recv_sem=self.recv.at[slot], device_id=peer, device_id_type=MESH,
            )

        def copy(self, key, peer, slot):
            self.handle(key, len(self.started), slot, peer).start()
            self.started.append(key)

        def arrive(self, key, slot):
            self.handle(key, 0, slot, sibling).wait_recv()

        def share(self, relation):
            key = (relation, core, "mine")
            self.copy(key, sibling, 8 + relation)
            if self.split:
                self.copy(key, y_next if relation % 2 else y_prev, 16 + relation)

        def first(self):
            self.copy((0, core, "all"), sibling, 8)
            own = (0, core, "mine")
            self.copy(own, x_next, 1)
            self.copy(own, x_prev, 2)
            self.copy(own, zw_pair, 3)
            if self.direct:
                self.copy(own, x_far, 6)

        def second(self):
            for relation in (1, 2, 3):
                self.arrive((relation, core, "mine"), relation)
                self.share(relation)
            if not self.direct:
                self.copy((1, core, 0), x_next, 6)
                self.copy((2, core, 1), x_prev, 0)
            self.copy((3, core, "mine"), x_next, 4)
            self.copy((3, core, "mine"), x_prev, 5)
            if self.direct:
                self.third()

        def third(self):
            if self.direct:
                self.arrive((6, core, "mine"), 6)
            else:
                self.arrive((6, core, 0), 6)
                self.arrive((6, core, 1), 0)
            self.share(6)
            self.copy((6, core, "mine"), zw_pair, 7)

        def fourth(self):
            for relation in (4, 5, 7):
                self.arrive((relation, core, "mine"), relation)
                self.share(relation)

        def fifth(self):
            for relation in range(1, 8):
                self.arrive((relation, core, "other"), 16 + relation)
                self.copy((relation, core, "other"), sibling, 24 + relation)

        def last(self):
            self.arrive((0, 1 - core, "all"), 8)
            for relation in range(1, 8):
                self.arrive((relation, 1 - core, "mine"), 8 + relation)
                if self.split:
                    self.arrive((relation, 1 - core, "other"), 24 + relation)

        def sent(self):
            for index, key in enumerate(self.started):
                self.handle(key, index, 0, sibling).wait_send()

    gather_a = Gather(w_a, wq.shape[0], a_send, a_recv, True, True)
    gather_b = Gather(w_b, wu.shape[0], b_send, b_recv, False, False)
    gather_c = Gather(w_c, wd.shape[0], c_send, c_recv, True, False)

    own48 = pl.ds(pl.multiple_of(slide * wq.shape[0], 16), wq.shape[0])
    w_a[own48, 0:width] = wq[...]
    w_a[own48, width:] = wkv[...]
    def grid(shape, dim):
        return lax.broadcasted_iota(jnp.int32, shape, dim)

    slots = tile_slot[...]
    devices = slides * ctxs
    share = block // devices
    owned = jnp.where((slots >> 9) == grid((devices, block), 0), 1.0, 0.0)
    earlier = jnp.where(grid((block, block), 0) < grid((block, block), 1), 1.0, 0.0).astype(bf16)
    ahead = dot(owned.astype(bf16), earlier)
    first_row = (grid((devices, block), 0) * share).astype(f32)
    target = jnp.sum(owned * (first_row + ahead), axis=0, keepdims=True)
    sorting = jnp.where(grid((block, block), 0).astype(f32) == target, 1.0, 0.0).astype(bf16)
    lane = grid((128, block), 0)
    digits = jnp.where(lane == 0, (slots >> 6) & 63, jnp.where(lane == 1, slots & 63, 0))
    outgoing[:, 0:width] = dot(sorting, tile_rows[...]).astype(bf16)
    outgoing[:, width:] = dot_nt(sorting, digits.astype(f32).astype(bf16)).astype(bf16)

    pl.semaphore_wait(barrier, len(work_peers) + len(near))
    gather_a.first()
    lengths[0] = jnp.full(lengths.shape[1:], length_ref[0], jnp.int32)

    def length_handle():
        return pltpu.make_async_remote_copy(
            src_ref=lengths.at[0], dst_ref=lengths.at[1], send_sem=l_sem.at[0],
            recv_sem=l_sem.at[1], device_id=sibling, device_id_type=MESH,
        )

    length_handle().start()

    def pieces(buffer, index, depth):
        return buffer.at[pl.ds(pl.multiple_of(index * depth, 16), depth), :]

    slide_rows = block // slides

    def to_work(by):
        return pltpu.make_async_remote_copy(
            src_ref=pieces(outgoing, lax.rem(work + by, slides), slide_rows),
            dst_ref=pieces(in_slide, work, slide_rows), send_sem=s_send.at[by],
            recv_sem=s_recv.at[by], device_id=work_peers[by - 1], device_id_type=MESH,
        )

    def from_work(by):
        part = pieces(in_slide, lax.rem(work + slides - by, slides), slide_rows)
        return pltpu.make_async_remote_copy(
            src_ref=part, dst_ref=part, send_sem=s_send.at[by],
            recv_sem=s_recv.at[by], device_id=work_peers[by - 1], device_id_type=MESH,
        )

    for by in range(1, slides):
        to_work(by).start()
    own32 = pl.ds(pl.multiple_of(work * slide_rows, 16), slide_rows)
    in_slide[own32, :] = outgoing[own32, :]

    w_b[own48, 0:width] = wo[...]
    w_b[own48, width:] = wu[...]
    own192 = pl.ds(pl.multiple_of(slide * wd.shape[0], 16), wd.shape[0])
    w_c[own192, :] = wd[...]
    eye[...] = identity(width)
    q_aug[...] = jnp.zeros(q_aug.shape, bf16)
    q_aug[:, 128:144, :] = jnp.where(grid((pairs, 16, 2 * block), 1) == 0, 1.0, 0.0).astype(bf16)
    for v_buf in (v_even, v_odd):
        v_buf[:, 64:80, :] = jnp.where(grid((heads, 16, block), 1) == 0, 1.0, 0.0).astype(bf16)
    top[...] = jnp.full(top.shape, masked_score, f32)
    acc[...] = jnp.zeros(acc.shape, f32)

    gather_a.second()
    gather_a.fourth()

    for by in range(1, slides):
        from_work(by).wait_recv()
    wanted = grid((block, block), 0)
    wanted = ((wanted >> 2) & 15) * slide_rows + (wanted >> 6) * share + (wanted & 3)
    turning = jnp.where(grid((block, block), 1) == wanted, 1.0, 0.0).astype(bf16)
    by_ctx[...] = dot(turning, in_slide[...]).astype(bf16)

    place = {key: index for index, key in enumerate(ORDER)}

    def chunk(relation, side):
        return rows.at[pl.ds(place[relation, side] * half, half), :]

    token_sends = []

    def rows_handle(source, target, send_slot, peer):
        return pltpu.make_async_remote_copy(
            src_ref=chunk(*source), dst_ref=chunk(*target), send_sem=t_send.at[send_slot],
            recv_sem=t_recv.at[place[target]], device_id=peer, device_id_type=MESH,
        )

    def pass_rows(source, relation, side, peer):
        rows_handle(source, (relation, side), len(token_sends), peer).start()
        token_sends.append(source)

    def rows_here(relation, side):
        rows_handle((relation, side), (relation, side), 0, sibling).wait_recv()

    for side in range(2):
        part = slice(side * half, (side + 1) * half)
        rows[part, :] = layer_norm(by_ctx[part, 0:width], gain1[...])
        pass_rows((0, side), 4, side, sibling)
        if side == 0:
            pass_rows((0, 0), 1, 0, y_next)
        else:
            pass_rows((0, 1), 2, 1, y_prev)

    def positions(buffer):
        weight = grid((8, 128), 1)
        weight = jnp.where(weight == 0, 64.0, jnp.where(weight == 1, 1.0, 0.0)).astype(bf16)
        return dot_nt(weight, buffer[:, width:])

    length_handle().wait()
    valid = jnp.where(core == z_lo, lengths[0, 0:1, 0:1], lengths[1, 0:1, 0:1]).astype(f32)
    masked = jnp.where(positions(by_ctx) >= valid, masked_score, 0.0)
    masks[member, 0] = masked[:, 0:half]
    masks[member, 1] = masked[:, half:]

    def mask_handle(by, owner):
        return pltpu.make_async_remote_copy(
            src_ref=masks.at[owner], dst_ref=masks.at[owner], send_sem=m_send.at[by],
            recv_sem=m_recv.at[by], device_id=members[by - 1], device_id_type=MESH,
        )

    for by in range(1, ctxs):
        mask_handle(by, member).start()

    gather_a.fifth()
    gather_b.first()
    gather_a.last()
    w_vt[...] = dot_nt(eye[...], w_a[:, 2 * width :]).astype(bf16)

    k_bufs, v_bufs, biases = (k_even, k_odd), (v_even, v_odd), (bias_even, bias_odd)

    def project(step, third, parity):
        here = rows[pl.ds(pl.multiple_of(step * block, block), block), :]
        span = pl.ds(pl.multiple_of(third * 256, 256), 256)
        key_span = pl.ds(pl.multiple_of(width + third * 256, 256), 256)
        k_bufs[parity][:, span] = dot(here, w_a[:, key_span]).astype(bf16)
        values_t = dot_nt(w_vt[span, :], here).astype(bf16)
        for at in range(4):
            v_bufs[parity][4 * third + at, 0:64, :] = values_t[at * 64 : at * 64 + 64, :]

    for third in range(3):
        project(0, third, 0)

    scale = HEAD_DIM ** (-0.5) * 1.4426950408889634
    queries = (dot(rows[0:block, :], w_a[:, 0:width]) * scale).astype(bf16)
    queries_t = dot_nt(eye[...], queries).astype(bf16)
    for head in range(heads):
        pair, at = head // 2, head % 2
        q_aug[pair, at * 64 : at * 64 + 64, at * block : (at + 1) * block] = queries_t[
            head * 64 : head * 64 + 64, :
        ]

    for by in range(1, ctxs):
        mask_handle(by, lax.rem(member + ctxs - by, ctxs)).wait_recv()

    def owner(relation):
        yy = lax.rem(y + {0: 0, 1: 3, 2: 1, 3: 2}[relation % 4], 4)
        return yy * 2 + ((1 - core) if relation >= 4 else core)

    def mask_column(first, first_side, second, second_side, parity):
        here = jnp.concatenate([masks[first, first_side], masks[second, second_side]], axis=1)
        here = jnp.concatenate([here, jnp.zeros((120, block), f32)], axis=0).astype(bf16)
        biases[parity][...] = dot_nt(eye[0:block, 0:block], here).astype(bf16)

    def score(pair, slot, parity):
        keys = k_bufs[parity][:, pl.ds(pl.multiple_of(pair * 128, 128), 128)]
        scores[slot] = dot(jnp.concatenate([keys, biases[parity][...]], axis=1), q_aug[pair])

    def soften(pair, slot, parity):
        before = top[pair]
        now = jnp.maximum(before, jnp.max(scores[slot], axis=0, keepdims=True))
        factor = jnp.exp2(before - now)
        top[pair] = now
        for side in range(2):
            span = slice(side * block, (side + 1) * block)
            weights = jnp.exp2(scores[slot, :, span] - now[:, span]).astype(bf16)
            head = 2 * pair + side
            acc[head] = acc[head] * factor[:, span] + dot(v_bufs[parity][head], weights)

    steps = len(ORDER) // 2
    firsts = [owner(ORDER[2 * step][0]) for step in range(steps)]
    seconds = [owner(ORDER[2 * step + 1][0]) for step in range(steps)]
    first_sides = [ORDER[2 * step][1] for step in range(steps)]
    second_sides = [ORDER[2 * step + 1][1] for step in range(steps)]

    def pick(options, step):
        chosen = options[0]
        for index in range(1, len(options)):
            chosen = jnp.where(step == index, options[index], chosen)
        return chosen

    def mask_of(step, parity):
        mask_column(
            pick(firsts, step), pick(first_sides, step), pick(seconds, step), pick(second_sides, step),
            parity,
        )

    def step_0():
        rows_here(4, 0)
        rows_here(4, 1)
        pass_rows((0, 1), 1, 1, y_next)
        pass_rows((0, 0), 2, 0, y_prev)
        gather_c.first()

    def step_1():
        rows_here(1, 0)
        pass_rows((1, 0), 5, 0, sibling)
        pass_rows((1, 0), 3, 0, y_next)
        rows_here(2, 1)
        pass_rows((2, 1), 6, 1, sibling)
        pass_rows((2, 1), 3, 1, y_prev)

    def step_2():
        rows_here(5, 0)
        rows_here(6, 1)
        gather_b.second()

    def step_3():
        rows_here(1, 1)
        pass_rows((1, 1), 5, 1, sibling)
        rows_here(2, 0)
        pass_rows((2, 0), 6, 0, sibling)

    def step_4():
        rows_here(5, 1)
        rows_here(6, 0)
        gather_c.second()

    def step_5():
        rows_here(3, 0)
        pass_rows((3, 0), 7, 0, sibling)
        rows_here(3, 1)
        pass_rows((3, 1), 7, 1, sibling)

    def step_6():
        rows_here(7, 0)
        rows_here(7, 1)
        gather_b.third()

    def step_7():
        pass

    events = [step_0, step_1, step_2, step_3, step_4, step_5, step_6, step_7]

    def turn(step, parity):
        for index in range(parity, steps, 2):
            pl.when(step == index)(events[index])
        later = jnp.minimum(step + 1, steps - 1)
        mask_of(later, 1 - parity)

        for third in range(3):
            project(later, third, 1 - parity)
            score(2 * third + 1, 1, parity)
            soften(2 * third, 0, parity)
            if third < 2:
                score(2 * third + 2, 0, parity)
            else:
                score(0, 0, 1 - parity)
            soften(2 * third + 1, 1, parity)

    def two_steps(index, _):
        turn(2 * index, 0)
        turn(2 * index + 1, 1)
        return 0

    mask_of(0, 0)
    score(0, 0, 0)
    lax.fori_loop(0, steps // 2, two_steps, 0)

    gather_b.fourth()
    gather_c.fourth()
    for head in range(heads):
        done = acc[head]
        attended[head * 64 : head * 64 + 64, :] = (done[0:64] / done[64:65]).astype(bf16)
    gather_b.last()
    turned = dot_nt(eye[0:block, 0:block], attended[...]).astype(bf16)
    mid = (by_ctx[:, 0:width].astype(f32) + dot(turned, w_b[:, 0:width])).astype(bf16)
    for index, source in enumerate(token_sends):
        rows_handle(source, source, index, sibling).wait_send()
    rows[0:block, :] = layer_norm(mid, gain2[...])
    down_acc[...] = mid.astype(f32)
    finished[:, width:] = by_ctx[:, width:]
    gather_c.last()

    tile = up_buf.shape[2]
    tiles = hidden // tile
    part_rows = block // 4
    ctx_rows = block // ctxs

    def send_home(target_ctx):
        return pltpu.make_async_remote_copy(
            src_ref=pieces(finished, target_ctx, ctx_rows), dst_ref=pieces(landed, member, ctx_rows),
            send_sem=f_send.at[target_ctx], recv_sem=f_recv.at[member],
            device_id=(at_slide(z_hi, x, z_lo), target_ctx), device_id_type=MESH,
        )

    def from_member(index):
        part = pieces(landed, index, ctx_rows)
        return pltpu.make_async_remote_copy(
            src_ref=part, dst_ref=part, send_sem=f_send.at[index], recv_sem=f_recv.at[index],
            device_id=sibling, device_id_type=MESH,
        )

    stays = core == z_lo

    def piece(index, _):
        yy = lax.rem(y + pick([2, 1, 3, 0], index), 4)
        here = pl.ds(pl.multiple_of(yy * part_rows, part_rows), part_rows)

        def up(at, slot):
            span = pl.ds(pl.multiple_of(width + at * tile, 128), tile)
            up_buf[slot] = dot(rows[here, :], w_b[:, span])

        def down(at, slot):
            active = jax.nn.gelu(up_buf[slot], approximate=True).astype(bf16)
            span = pl.ds(pl.multiple_of(at * tile, tile), tile)
            down_acc[here, :] += dot(active, w_c[span, :])

        up(0, 0)

        def two_tiles(at, _):
            up(2 * at + 1, 1)
            down(2 * at, 0)
            up(jnp.minimum(2 * at + 2, tiles - 1), 0)
            down(2 * at + 1, 1)
            return 0

        lax.fori_loop(0, tiles // 2, two_tiles, 0)
        finished[here, 0:width] = down_acc[here, :].astype(bf16)
        for zz in range(2):
            target = yy * 2 + zz
            home = stays & (yy == y) & (z_lo == zz)

            @pl.when(jnp.logical_not(home))
            def _():
                send_home(target).start()

            @pl.when(home)
            def _():
                at = pl.ds(pl.multiple_of(member * ctx_rows, 16), ctx_rows)
                landed[at, :] = finished[pl.ds(pl.multiple_of(target * ctx_rows, 16), ctx_rows), :]

        return 0

    lax.fori_loop(0, 4, piece, 0)

    for index in range(ctxs):
        @pl.when(jnp.logical_not(stays & (member == index)))
        def _():
            from_member(index).wait_recv()

    at_row = positions(landed)[0:1] - (ctx * block).astype(f32)
    placing = jnp.where(grid((block, block), 0).astype(f32) == at_row, 1.0, 0.0).astype(bf16)
    at = ctx * block + grid((block, width), 0)
    out[...] = jnp.where(at < length_ref[0], dot(placing, landed[:, 0:width]), 0.0).astype(bf16)

    for index in range(ctxs):
        @pl.when(jnp.logical_not(stays & (ctx == index)))
        def _():
            send_home(index).wait_send()

    for by in range(1, slides):
        to_work(by).wait_send()
    for by in range(1, ctxs):
        mask_handle(by, member).wait_send()
    for gather in (gather_a, gather_b, gather_c):
        gather.sent()


def on_device(
    tile_rows, tile_slot, lengths, ln_gain_attn, w_query, w_kv, w_out, ln_gain_mlp, w_up, w_down
):
    block, width = tile_rows.shape
    heads = width // HEAD_DIM
    hidden = w_up.shape[1]
    vmem = pl.BlockSpec(memory_space=pltpu.VMEM)
    dma = pltpu.SemaphoreType.DMA
    return pl.pallas_call(
        layer_kernel,
        out_shape=jax.ShapeDtypeStruct((block, width), bf16),
        in_specs=[vmem, vmem, pl.BlockSpec(memory_space=pltpu.SMEM)] + [vmem] * 7,
        out_specs=vmem,
        scratch_shapes=[
            pltpu.VMEM((block, width + 128), bf16),
            pltpu.VMEM((block, width + 128), bf16),
            pltpu.VMEM((block, width + 128), bf16),
            pltpu.VMEM((block, width + 128), bf16),
            pltpu.VMEM((block, width + 128), bf16),
            pltpu.VMEM((2, 8, 128), jnp.int32),
            pltpu.VMEM((8, 2, 8, block // 2), f32),
            pltpu.VMEM((width, width), bf16),
            pltpu.VMEM((8 * block, width), bf16),
            pltpu.VMEM((width, 3 * width), bf16),
            pltpu.VMEM((width, width + hidden), bf16),
            pltpu.VMEM((hidden, width), bf16),
            pltpu.VMEM((width, width), bf16),
            pltpu.VMEM((heads // 2, 256, 2 * block), bf16),
            pltpu.VMEM((block, width), bf16),
            pltpu.VMEM((block, width), bf16),
            pltpu.VMEM((heads, value_rows, block), bf16),
            pltpu.VMEM((heads, value_rows, block), bf16),
            pltpu.VMEM((block, 128), bf16),
            pltpu.VMEM((block, 128), bf16),
            pltpu.VMEM((2, block, 2 * block), f32),
            pltpu.VMEM((heads // 2, 1, 2 * block), f32),
            pltpu.VMEM((heads, value_rows, block), f32),
            pltpu.VMEM((width, block), bf16),
            pltpu.VMEM((2, block // 4, 512), f32),
            pltpu.VMEM((block, width), f32),
            dma((16,)), dma((16,)),
            dma((8,)), dma((8,)),
            dma((8,)), dma((8,)),
            dma((2,)),
            dma((14,)), dma((16,)),
            dma((32,)), dma((32,)),
            dma((16,)), dma((16,)),
            dma((16,)), dma((16,)),
        ],
        compiler_params=pltpu.CompilerParams(
            collective_id=0, has_side_effects=True, vmem_limit_bytes=60 * 2**20
        ),
        name="layer",
    )(
        tile_rows, tile_slot, lengths, ln_gain_attn, w_query, w_kv, w_out,
        ln_gain_mlp, w_up, w_down,
    )


def solution(mesh):
    return jax.shard_map(
        on_device,
        mesh=mesh,
        in_specs=(
            P(("slide", "ctx"), None),
            P(("slide", "ctx"), None),
            P("slide"),
            P(),
            P("slide", None),
            P("slide", None),
            P("slide", None),
            P(),
            P("slide", None),
            P("slide", None),
        ),
        out_specs=P(("slide", "ctx"), None),
        check_vma=False,
    )
```

```python
import functools

import jax
import jax.numpy as jnp
from jax import lax
from jax.experimental import pallas as pl
from jax.experimental.pallas import tpu as pltpu
from jax.sharding import PartitionSpec as P

HEAD_DIM = 64
MESH = pl.DeviceIdType.MESH
bf16, f32 = jnp.bfloat16, jnp.float32

norm_eps = 1e-05
masked_score = -1e30
value_rows = 80
ORDER = [
    (0, 0), (0, 1), (4, 0), (4, 1), (1, 0), (2, 1), (5, 0), (6, 1),
    (1, 1), (2, 0), (5, 1), (6, 0), (3, 0), (3, 1), (7, 0), (7, 1),
]


def layer_norm(rows, gain):
    values32 = rows.astype(f32)
    row_mean = jnp.mean(values32, axis=-1, keepdims=True)
    centred = values32 - row_mean
    row_var = jnp.mean(centred * centred, axis=-1, keepdims=True)
    return (centred * lax.rsqrt(row_var + norm_eps) * gain).astype(bf16)


def dot(left, right):
    return jnp.dot(left, right, preferred_element_type=f32)


def dot_nt(left, right):
    return lax.dot_general(left, right, (((1,), (1,)), ((), ())), preferred_element_type=f32)


def identity(size):
    row = lax.broadcasted_iota(jnp.int32, (size, size), 0)
    column = lax.broadcasted_iota(jnp.int32, (size, size), 1)
    return jnp.where(row == column, 1.0, 0.0).astype(bf16)


def layer_kernel(
    tile_rows, tile_slot, length_ref, gain1, wq, wkv, wo, gain2, wu, wd,
    out,
    outgoing, in_slide, by_ctx, finished, landed, landed_at, lengths, masks, eye,
    rows, w_a, w_b, w_c, w_vt, q_aug, k_even, k_odd, v_even, v_odd, bias_even, bias_odd, scores, top, acc, attended, up_buf, down_acc,
    s_send, s_recv, f_send, f_recv, i_send, i_recv, m_send, m_recv, l_sem, t_send, t_recv, a_send, a_recv, b_send, b_recv, c_send, c_recv,
):
    block, width = tile_rows.shape
    half = block // 2
    heads = width // HEAD_DIM
    pairs = heads // 2
    hidden = wu.shape[1]
    slide = lax.axis_index("slide")
    ctx = lax.axis_index("ctx")
    z_hi, x, core = lax.div(slide, 8), lax.rem(lax.div(slide, 2), 4), lax.rem(slide, 2)
    y, z_lo = lax.div(ctx, 2), lax.rem(ctx, 2)

    def at_slide(zz, xx, cc):
        return zz * 8 + lax.rem(xx + 4, 4) * 2 + cc

    def at_ctx(yy, zz):
        return lax.rem(yy + 4, 4) * 2 + zz

    slides, ctxs = 16, 8
    y_next = (slide, at_ctx(y + 1, z_lo))
    y_prev = (slide, at_ctx(y - 1, z_lo))
    x_next = (at_slide(z_hi, x + 1, core), ctx)
    x_prev = (at_slide(z_hi, x - 1, core), ctx)
    zw_pair = (at_slide(1 - z_hi, x, core), at_ctx(y, 1 - z_lo))
    sibling = (at_slide(z_hi, x, 1 - core), ctx)

    work = at_slide(z_hi, x, z_lo)
    member = y * 2 + core

    def works_on(index):
        return (
            at_slide(lax.div(index, 8), lax.rem(lax.div(index, 2), 4), core),
            at_ctx(y, lax.rem(index, 2)),
        )

    def at_member(index):
        return (at_slide(z_hi, x, lax.rem(index, 2)), at_ctx(lax.div(index, 2), z_lo))

    work_peers = [works_on(lax.rem(work + by, slides)) for by in range(1, slides)]
    members = [at_member(lax.rem(member + by, ctxs)) for by in range(1, ctxs)]
    near = [
        (at_slide(z_hi, x, lax.rem(core + c, 2)), at_ctx(y + yy, lax.rem(z_lo + zz, 2)))
        for c in range(2) for yy in range(4) for zz in range(2) if (c, yy) != (0, 0)
    ]
    barrier = pltpu.get_barrier_semaphore()
    for peer in work_peers + near:
        pl.semaphore_signal(barrier, inc=1, device_id=peer, device_id_type=MESH)

    def shard_of(relation, cc):
        zz = (1 - z_hi) if relation in (3, 4, 5, 7) else z_hi
        step = {0: 0, 1: -1, 2: 1, 3: 0, 4: -1, 5: 1, 6: 2, 7: 2}[relation]
        return at_slide(zz, x + step, cc)

    x_far = (at_slide(z_hi, x + 2, core), ctx)

    class Gather:
        def __init__(self, whole, depth, send, recv, direct, split):
            self.whole, self.depth, self.send, self.recv = whole, depth, send, recv
            self.direct, self.split = direct, split
            self.started = []

        def part(self, relation, cc, columns):
            at = pl.ds(pl.multiple_of(shard_of(relation, cc) * self.depth, 16), self.depth)
            cut = self.whole.shape[1] // 2
            if columns == "all" or (columns == "mine" and not self.split):
                return self.whole.at[at, :]
            if columns in (0, 1):
                return self.whole.at[at, pl.ds(columns * cut, cut)]
            side = lax.rem(y, 2) if columns == "mine" else 1 - lax.rem(y, 2)
            return self.whole.at[at, pl.ds(pl.multiple_of(side * cut, 128), cut)]

        def handle(self, key, send_slot, slot, peer):
            part = self.part(*key)
            return pltpu.make_async_remote_copy(
                src_ref=part, dst_ref=part, send_sem=self.send.at[send_slot],
                recv_sem=self.recv.at[slot], device_id=peer, device_id_type=MESH,
            )

        def copy(self, key, peer, slot):
            self.handle(key, len(self.started), slot, peer).start()
            self.started.append(key)

        def arrive(self, key, slot):
            self.handle(key, 0, slot, sibling).wait_recv()

        def share(self, relation):
            key = (relation, core, "mine")
            self.copy(key, sibling, 8 + relation)
            if self.split:
                self.copy(key, y_next if relation % 2 else y_prev, 16 + relation)

        def first(self):
            self.copy((0, core, "all"), sibling, 8)
            own = (0, core, "mine")
            self.copy(own, x_next, 1)
            self.copy(own, x_prev, 2)
            self.copy(own, zw_pair, 3)
            if self.direct:
                self.copy(own, x_far, 6)

        def second(self):
            for relation in (1, 2, 3):
                self.arrive((relation, core, "mine"), relation)
                self.share(relation)
            if not self.direct:
                self.copy((1, core, 0), x_next, 6)
                self.copy((2, core, 1), x_prev, 0)
            self.copy((3, core, "mine"), x_next, 4)
            self.copy((3, core, "mine"), x_prev, 5)
            if self.direct:
                self.third()

        def third(self):
            if self.direct:
                self.arrive((6, core, "mine"), 6)
            else:
                self.arrive((6, core, 0), 6)
                self.arrive((6, core, 1), 0)
            self.share(6)
            self.copy((6, core, "mine"), zw_pair, 7)

        def fourth(self):
            for relation in (4, 5, 7):
                self.arrive((relation, core, "mine"), relation)
                self.share(relation)

        def fifth(self):
            for relation in range(1, 8):
                self.arrive((relation, core, "other"), 16 + relation)
                self.copy((relation, core, "other"), sibling, 24 + relation)

        def last(self):
            self.arrive((0, 1 - core, "all"), 8)
            for relation in range(1, 8):
                self.arrive((relation, 1 - core, "mine"), 8 + relation)
                if self.split:
                    self.arrive((relation, 1 - core, "other"), 24 + relation)

        def sent(self):
            for index, key in enumerate(self.started):
                self.handle(key, index, 0, sibling).wait_send()

    gather_a = Gather(w_a, wq.shape[0], a_send, a_recv, True, True)
    gather_b = Gather(w_b, wu.shape[0], b_send, b_recv, False, False)
    gather_c = Gather(w_c, wd.shape[0], c_send, c_recv, True, False)

    own48 = pl.ds(pl.multiple_of(slide * wq.shape[0], 16), wq.shape[0])
    w_a[own48, 0:width] = wq[...]
    w_a[own48, width:] = wkv[...]
    def grid(shape, dim):
        return lax.broadcasted_iota(jnp.int32, shape, dim)

    slots = tile_slot[...]
    devices = slides * ctxs
    share = block // devices
    owned = jnp.where((slots >> 9) == grid((devices, block), 0), 1.0, 0.0)
    earlier = jnp.where(grid((block, block), 0) < grid((block, block), 1), 1.0, 0.0).astype(bf16)
    ahead = dot(owned.astype(bf16), earlier)
    first_row = (grid((devices, block), 0) * share).astype(f32)
    target = jnp.sum(owned * (first_row + ahead), axis=0, keepdims=True)
    sorting = jnp.where(grid((block, block), 0).astype(f32) == target, 1.0, 0.0).astype(bf16)
    lane = grid((128, block), 0)
    digits = jnp.where(lane == 0, (slots >> 6) & 63, jnp.where(lane == 1, slots & 63, 0))
    outgoing[:, 0:width] = dot(sorting, tile_rows[...]).astype(bf16)
    outgoing[:, width:] = dot_nt(sorting, digits.astype(f32).astype(bf16)).astype(bf16)

    pl.semaphore_wait(barrier, len(work_peers) + len(near))
    gather_a.first()
    lengths[0] = jnp.full(lengths.shape[1:], length_ref[0], jnp.int32)

    def length_handle():
        return pltpu.make_async_remote_copy(
            src_ref=lengths.at[0], dst_ref=lengths.at[1], send_sem=l_sem.at[0],
            recv_sem=l_sem.at[1], device_id=sibling, device_id_type=MESH,
        )

    length_handle().start()

    def pieces(buffer, index, depth):
        return buffer.at[pl.ds(pl.multiple_of(index * depth, 16), depth), :]

    slide_rows = block // slides

    def to_work(by):
        return pltpu.make_async_remote_copy(
            src_ref=pieces(outgoing, lax.rem(work + by, slides), slide_rows),
            dst_ref=pieces(in_slide, work, slide_rows), send_sem=s_send.at[by],
            recv_sem=s_recv.at[by], device_id=work_peers[by - 1], device_id_type=MESH,
        )

    def from_work(by):
        part = pieces(in_slide, lax.rem(work + slides - by, slides), slide_rows)
        return pltpu.make_async_remote_copy(
            src_ref=part, dst_ref=part, send_sem=s_send.at[by],
            recv_sem=s_recv.at[by], device_id=work_peers[by - 1], device_id_type=MESH,
        )

    for by in range(1, slides):
        to_work(by).start()
    own32 = pl.ds(pl.multiple_of(work * slide_rows, 16), slide_rows)
    in_slide[own32, :] = outgoing[own32, :]

    w_b[own48, 0:width] = wo[...]
    w_b[own48, width:] = wu[...]
    own192 = pl.ds(pl.multiple_of(slide * wd.shape[0], 16), wd.shape[0])
    w_c[own192, :] = wd[...]
    eye[...] = identity(width)
    q_aug[...] = jnp.zeros(q_aug.shape, bf16)
    q_aug[:, 128:144, :] = jnp.where(grid((pairs, 16, 2 * block), 1) == 0, 1.0, 0.0).astype(bf16)
    for v_buf in (v_even, v_odd):
        v_buf[:, 64:80, :] = jnp.where(grid((heads, 16, block), 1) == 0, 1.0, 0.0).astype(bf16)
    top[...] = jnp.full(top.shape, masked_score, f32)
    acc[...] = jnp.zeros(acc.shape, f32)

    gather_a.second()
    gather_a.fourth()

    for by in range(1, slides):
        from_work(by).wait_recv()
    wanted = grid((block, block), 0)
    wanted = ((wanted >> 2) & 15) * slide_rows + (wanted >> 6) * share + (wanted & 3)
    turning = jnp.where(grid((block, block), 1) == wanted, 1.0, 0.0).astype(bf16)
    by_ctx[...] = dot(turning, in_slide[...]).astype(bf16)

    place = {key: index for index, key in enumerate(ORDER)}

    def chunk(relation, side):
        return rows.at[pl.ds(place[relation, side] * half, half), :]

    token_sends = []

    def rows_handle(source, target, send_slot, peer):
        return pltpu.make_async_remote_copy(
            src_ref=chunk(*source), dst_ref=chunk(*target), send_sem=t_send.at[send_slot],
            recv_sem=t_recv.at[place[target]], device_id=peer, device_id_type=MESH,
        )

    def pass_rows(source, relation, side, peer):
        rows_handle(source, (relation, side), len(token_sends), peer).start()
        token_sends.append(source)

    def rows_here(relation, side):
        rows_handle((relation, side), (relation, side), 0, sibling).wait_recv()

    for side in range(2):
        part = slice(side * half, (side + 1) * half)
        rows[part, :] = layer_norm(by_ctx[part, 0:width], gain1[...])
        pass_rows((0, side), 4, side, sibling)
        if side == 0:
            pass_rows((0, 0), 1, 0, y_next)
        else:
            pass_rows((0, 1), 2, 1, y_prev)

    def positions(buffer):
        weight = grid((8, 128), 1)
        weight = jnp.where(weight == 0, 64.0, jnp.where(weight == 1, 1.0, 0.0)).astype(bf16)
        return dot_nt(weight, buffer)

    length_handle().wait()
    valid = jnp.where(core == z_lo, lengths[0, 0:1, 0:1], lengths[1, 0:1, 0:1]).astype(f32)
    masked = jnp.where(positions(by_ctx[:, width:]) >= valid, masked_score, 0.0)
    masks[member, 0] = masked[:, 0:half]
    masks[member, 1] = masked[:, half:]

    def mask_handle(by, owner):
        return pltpu.make_async_remote_copy(
            src_ref=masks.at[owner], dst_ref=masks.at[owner], send_sem=m_send.at[by],
            recv_sem=m_recv.at[by], device_id=members[by - 1], device_id_type=MESH,
        )

    for by in range(1, ctxs):
        mask_handle(by, member).start()

    ctx_rows = block // ctxs
    stays = core == z_lo

    def send_places(target_ctx):
        at = pl.ds(pl.multiple_of(target_ctx * ctx_rows, 16), ctx_rows)
        return pltpu.make_async_remote_copy(
            src_ref=by_ctx.at[at, pl.ds(width, 128)], dst_ref=pieces(landed_at, member, ctx_rows),
            send_sem=i_send.at[target_ctx], recv_sem=i_recv.at[member],
            device_id=(at_slide(z_hi, x, z_lo), target_ctx), device_id_type=MESH,
        )

    for index in range(ctxs):
        @pl.when(jnp.logical_not(stays & (ctx == index)))
        def _():
            send_places(index).start()

    @pl.when(stays)
    def _():
        at = pl.ds(pl.multiple_of(member * ctx_rows, 16), ctx_rows)
        landed_at[at, :] = by_ctx[pl.ds(pl.multiple_of(ctx * ctx_rows, 16), ctx_rows), width:]

    gather_a.fifth()
    gather_b.first()
    gather_a.last()
    w_vt[...] = dot_nt(eye[...], w_a[:, 2 * width :]).astype(bf16)

    k_bufs, v_bufs, biases = (k_even, k_odd), (v_even, v_odd), (bias_even, bias_odd)

    def project(step, third, parity):
        here = rows[pl.ds(pl.multiple_of(step * block, block), block), :]
        span = pl.ds(pl.multiple_of(third * 256, 256), 256)
        key_span = pl.ds(pl.multiple_of(width + third * 256, 256), 256)
        k_bufs[parity][:, span] = dot(here, w_a[:, key_span]).astype(bf16)
        values_t = dot_nt(w_vt[span, :], here).astype(bf16)
        for at in range(4):
            v_bufs[parity][4 * third + at, 0:64, :] = values_t[at * 64 : at * 64 + 64, :]

    for third in range(3):
        project(0, third, 0)

    scale = HEAD_DIM ** (-0.5) * 1.4426950408889634
    queries = (dot(rows[0:block, :], w_a[:, 0:width]) * scale).astype(bf16)
    queries_t = dot_nt(eye[...], queries).astype(bf16)
    for head in range(heads):
        pair, at = head // 2, head % 2
        q_aug[pair, at * 64 : at * 64 + 64, at * block : (at + 1) * block] = queries_t[
            head * 64 : head * 64 + 64, :
        ]

    for by in range(1, ctxs):
        mask_handle(by, lax.rem(member + ctxs - by, ctxs)).wait_recv()

    def owner(relation):
        yy = lax.rem(y + {0: 0, 1: 3, 2: 1, 3: 2}[relation % 4], 4)
        return yy * 2 + ((1 - core) if relation >= 4 else core)

    def mask_column(first, first_side, second, second_side, parity):
        here = jnp.concatenate([masks[first, first_side], masks[second, second_side]], axis=1)
        here = jnp.concatenate([here, jnp.zeros((120, block), f32)], axis=0).astype(bf16)
        biases[parity][...] = dot_nt(eye[0:block, 0:block], here).astype(bf16)

    def score(pair, slot, parity):
        keys = k_bufs[parity][:, pl.ds(pl.multiple_of(pair * 128, 128), 128)]
        scores[slot] = dot(jnp.concatenate([keys, biases[parity][...]], axis=1), q_aug[pair])

    def soften(pair, slot, parity):
        before = top[pair]
        now = jnp.maximum(before, jnp.max(scores[slot], axis=0, keepdims=True))
        factor = jnp.exp2(before - now)
        top[pair] = now
        for side in range(2):
            span = slice(side * block, (side + 1) * block)
            weights = jnp.exp2(scores[slot, :, span] - now[:, span]).astype(bf16)
            head = 2 * pair + side
            acc[head] = acc[head] * factor[:, span] + dot(v_bufs[parity][head], weights)

    steps = len(ORDER) // 2
    firsts = [owner(ORDER[2 * step][0]) for step in range(steps)]
    seconds = [owner(ORDER[2 * step + 1][0]) for step in range(steps)]
    first_sides = [ORDER[2 * step][1] for step in range(steps)]
    second_sides = [ORDER[2 * step + 1][1] for step in range(steps)]

    def pick(options, step):
        chosen = options[0]
        for index in range(1, len(options)):
            chosen = jnp.where(step == index, options[index], chosen)
        return chosen

    def mask_of(step, parity):
        mask_column(
            pick(firsts, step), pick(first_sides, step), pick(seconds, step), pick(second_sides, step),
            parity,
        )

    def step_0():
        rows_here(4, 0)
        rows_here(4, 1)
        pass_rows((0, 1), 1, 1, y_next)
        pass_rows((0, 0), 2, 0, y_prev)
        gather_c.first()

    def step_1():
        rows_here(1, 0)
        pass_rows((1, 0), 5, 0, sibling)
        rows_here(2, 1)
        pass_rows((2, 1), 6, 1, sibling)

    def step_2():
        pass_rows((1, 0), 3, 0, y_next)
        pass_rows((2, 1), 3, 1, y_prev)
        rows_here(5, 0)
        rows_here(6, 1)
        gather_b.second()

    def step_3():
        rows_here(1, 1)
        pass_rows((1, 1), 5, 1, sibling)
        rows_here(2, 0)
        pass_rows((2, 0), 6, 0, sibling)

    def step_4():
        rows_here(5, 1)
        rows_here(6, 0)
        gather_c.second()

    def step_5():
        rows_here(3, 0)
        pass_rows((3, 0), 7, 0, sibling)
        rows_here(3, 1)
        pass_rows((3, 1), 7, 1, sibling)

    def step_6():
        rows_here(7, 0)
        rows_here(7, 1)
        gather_b.third()

    def step_7():
        pass

    events = [step_0, step_1, step_2, step_3, step_4, step_5, step_6, step_7]

    def turn(step, parity):
        for index in range(parity, steps, 2):
            pl.when(step == index)(events[index])
        later = jnp.minimum(step + 1, steps - 1)
        mask_of(later, 1 - parity)

        for third in range(3):
            project(later, third, 1 - parity)
            score(2 * third + 1, 1, parity)
            soften(2 * third, 0, parity)
            if third < 2:
                score(2 * third + 2, 0, parity)
            else:
                score(0, 0, 1 - parity)
            soften(2 * third + 1, 1, parity)

    def two_steps(index, _):
        turn(2 * index, 0)
        turn(2 * index + 1, 1)
        return 0

    mask_of(0, 0)
    score(0, 0, 0)
    lax.fori_loop(0, steps // 2, two_steps, 0)

    for head in range(heads):
        done = acc[head]
        attended[head * 64 : head * 64 + 64, :] = (done[0:64] / done[64:65]).astype(bf16)
    gather_b.fourth()
    gather_c.fourth()
    gather_b.last()
    turned = dot_nt(eye[0:block, 0:block], attended[...]).astype(bf16)
    mid = (by_ctx[:, 0:width].astype(f32) + dot(turned, w_b[:, 0:width])).astype(bf16)
    for index, source in enumerate(token_sends):
        rows_handle(source, source, index, sibling).wait_send()
    rows[0:block, :] = layer_norm(mid, gain2[...])
    down_acc[...] = mid.astype(f32)
    gather_c.last()

    tile = up_buf.shape[2]
    tiles = hidden // tile
    part_rows = block // 4

    def send_home(target_ctx):
        return pltpu.make_async_remote_copy(
            src_ref=pieces(finished, target_ctx, ctx_rows), dst_ref=pieces(landed, member, ctx_rows),
            send_sem=f_send.at[target_ctx], recv_sem=f_recv.at[member],
            device_id=(at_slide(z_hi, x, z_lo), target_ctx), device_id_type=MESH,
        )

    def from_member(index, buffer, send, recv):
        part = pieces(buffer, index, ctx_rows)
        return pltpu.make_async_remote_copy(
            src_ref=part, dst_ref=part, send_sem=send.at[index], recv_sem=recv.at[index],
            device_id=sibling, device_id_type=MESH,
        )

    def piece(index, _):
        yy = lax.rem(y + pick([2, 1, 3, 0], index), 4)
        here = pl.ds(pl.multiple_of(yy * part_rows, part_rows), part_rows)

        def up(at, slot):
            span = pl.ds(pl.multiple_of(width + at * tile, 128), tile)
            up_buf[slot] = dot(rows[here, :], w_b[:, span])

        def down(at, slot):
            active = jax.nn.gelu(up_buf[slot], approximate=True).astype(bf16)
            span = pl.ds(pl.multiple_of(at * tile, tile), tile)
            down_acc[here, :] += dot(active, w_c[span, :])

        up(0, 0)

        def two_tiles(at, _):
            up(2 * at + 1, 1)
            down(2 * at, 0)
            up(jnp.minimum(2 * at + 2, tiles - 1), 0)
            down(2 * at + 1, 1)
            return 0

        lax.fori_loop(0, tiles // 2, two_tiles, 0)
        finished[here, :] = down_acc[here, :].astype(bf16)
        for zz in range(2):
            target = yy * 2 + zz
            home = stays & (yy == y) & (z_lo == zz)

            @pl.when(jnp.logical_not(home))
            def _():
                send_home(target).start()

            @pl.when(home)
            def _():
                at = pl.ds(pl.multiple_of(member * ctx_rows, 16), ctx_rows)
                landed[at, :] = finished[pl.ds(pl.multiple_of(target * ctx_rows, 16), ctx_rows), :]

        return 0

    lax.fori_loop(0, 4, piece, 0)

    for index in range(ctxs):
        @pl.when(jnp.logical_not(stays & (member == index)))
        def _():
            from_member(index, landed_at, i_send, i_recv).wait_recv()
            from_member(index, landed, f_send, f_recv).wait_recv()

    at_row = positions(landed_at[...])[0:1] - (ctx * block).astype(f32)
    placing = jnp.where(grid((block, block), 0).astype(f32) == at_row, 1.0, 0.0).astype(bf16)
    at = ctx * block + grid((block, width), 0)
    out[...] = jnp.where(at < length_ref[0], dot(placing, landed[...]), 0.0).astype(bf16)

    for index in range(ctxs):
        @pl.when(jnp.logical_not(stays & (ctx == index)))
        def _():
            send_places(index).wait_send()
            send_home(index).wait_send()

    for by in range(1, slides):
        to_work(by).wait_send()
    for by in range(1, ctxs):
        mask_handle(by, member).wait_send()
    for gather in (gather_a, gather_b, gather_c):
        gather.sent()


def on_device(
    tile_rows, tile_slot, lengths, ln_gain_attn, w_query, w_kv, w_out, ln_gain_mlp, w_up, w_down
):
    block, width = tile_rows.shape
    heads = width // HEAD_DIM
    hidden = w_up.shape[1]
    vmem = pl.BlockSpec(memory_space=pltpu.VMEM)
    dma = pltpu.SemaphoreType.DMA
    return pl.pallas_call(
        layer_kernel,
        out_shape=jax.ShapeDtypeStruct((block, width), bf16),
        in_specs=[vmem, vmem, pl.BlockSpec(memory_space=pltpu.SMEM)] + [vmem] * 7,
        out_specs=vmem,
        scratch_shapes=[
            pltpu.VMEM((block, width + 128), bf16),
            pltpu.VMEM((block, width + 128), bf16),
            pltpu.VMEM((block, width + 128), bf16),
            pltpu.VMEM((block, width), bf16),
            pltpu.VMEM((block, width), bf16),
            pltpu.VMEM((block, 128), bf16),
            pltpu.VMEM((2, 8, 128), jnp.int32),
            pltpu.VMEM((8, 2, 8, block // 2), f32),
            pltpu.VMEM((width, width), bf16),
            pltpu.VMEM((8 * block, width), bf16),
            pltpu.VMEM((width, 3 * width), bf16),
            pltpu.VMEM((width, width + hidden), bf16),
            pltpu.VMEM((hidden, width), bf16),
            pltpu.VMEM((width, width), bf16),
            pltpu.VMEM((heads // 2, 256, 2 * block), bf16),
            pltpu.VMEM((block, width), bf16),
            pltpu.VMEM((block, width), bf16),
            pltpu.VMEM((heads, value_rows, block), bf16),
            pltpu.VMEM((heads, value_rows, block), bf16),
            pltpu.VMEM((block, 128), bf16),
            pltpu.VMEM((block, 128), bf16),
            pltpu.VMEM((2, block, 2 * block), f32),
            pltpu.VMEM((heads // 2, 1, 2 * block), f32),
            pltpu.VMEM((heads, value_rows, block), f32),
            pltpu.VMEM((width, block), bf16),
            pltpu.VMEM((2, block // 4, 512), f32),
            pltpu.VMEM((block, width), f32),
            dma((16,)), dma((16,)),
            dma((8,)), dma((8,)),
            dma((8,)), dma((8,)),
            dma((8,)), dma((8,)),
            dma((2,)),
            dma((14,)), dma((16,)),
            dma((32,)), dma((32,)),
            dma((16,)), dma((16,)),
            dma((16,)), dma((16,)),
        ],
        compiler_params=pltpu.CompilerParams(
            collective_id=0, has_side_effects=True, vmem_limit_bytes=60 * 2**20
        ),
        name="layer",
    )(
        tile_rows, tile_slot, lengths, ln_gain_attn, w_query, w_kv, w_out,
        ln_gain_mlp, w_up, w_down,
    )


def solution(mesh):
    return jax.shard_map(
        on_device,
        mesh=mesh,
        in_specs=(
            P(("slide", "ctx"), None),
            P(("slide", "ctx"), None),
            P("slide"),
            P(),
            P("slide", None),
            P("slide", None),
            P("slide", None),
            P(),
            P("slide", None),
            P("slide", None),
        ),
        out_specs=P(("slide", "ctx"), None),
        check_vma=False,
    )
```
